32 devices in a mesh: ctx: 16 (over z, y, core), chan: 2 (over x).
Axes of the slice: x: 2, y: 2, z: 4, core: 2. Of those that a mesh axis runs over, the one named last changes fastest.
Arguments:
- query_in: bfloat16 [2048, 1024], P('ctx', 'chan'), may hold values from -6 to 6
- key_in: bfloat16 [2048, 1024], P('ctx', 'chan'), may hold values from -6 to 6
- value_in: bfloat16 [2048, 1024], P('ctx', 'chan'), may hold values from -6 to 6
- grad_out: bfloat16 [2048, 1024], P('ctx', 'chan'), may hold values from -6 to 6
- residue: float32 [16, 1024], P(None, 'chan'), may hold values from -0.34 to 0.34
- decay_rate: float32 [16, 1024], P(None, 'chan'), may hold values from 4.39453125e-05 to 0.05
Outputs:
- grad_query: bfloat16 [2048, 1024], P('ctx', 'chan')
- grad_key: bfloat16 [2048, 1024], P('ctx', 'chan')
- grad_value: bfloat16 [2048, 1024], P('ctx', 'chan')
- grad_residue: float32 [16, 1024], P(None, 'chan')
- grad_log_rate: float32 [16, 1024], P(None, 'chan')
- filter_norm: float32 [], replicated
The draws below stay inside these ranges and needn't reach their ends.
All inputs are finite; a program needn't handle non-finite values.
Results may differ from the reference program's by a relative error of at most 0.003.
Values may be sent and summed in bfloat16 or wider, within the bound.
A program may use at most 64 MiB of HBM per device.

```python
import math
import jax
import jax.numpy as jnp
from jax import lax

CH = 1024
M = 16
SEQ = 2048


def rate_table(key, slow_share):
    picker = jax.random.uniform(jax.random.fold_in(key, 11), (M, CH), jnp.float32)
    slow_rates = jnp.exp(jax.random.uniform(jax.random.fold_in(key, 12), (M, CH), jnp.float32, math.log(0.1), math.log(2.0))) / SEQ
    fast_rates = jnp.exp(jax.random.uniform(jax.random.fold_in(key, 13), (M, CH), jnp.float32, math.log(0.02), math.log(0.05)))
    return jnp.where(picker < slow_share, slow_rates, fast_rates)


def draw_decay_rate(key, part):
    share = 0.5
    rates = rate_table(key, share)
    return rates.astype(jnp.float32)


def draw_residue(key, part):
    share = 0.5
    rates = rate_table(key, share)
    key = jax.random.fold_in(key, 5)
    noise = jax.random.truncated_normal(key, -4.0, 4.0, (M, CH), jnp.float32)
    return (noise * jnp.sqrt(2.0 * rates + 2.0 / SEQ) / math.sqrt(M)).astype(jnp.float32)


def level_of(stream_key, extent, shards, low, largest):
    def one(axis_at, blocks):
        draws = jax.random.uniform(jax.random.fold_in(jax.random.fold_in(stream_key, 6), axis_at), (blocks,), jnp.float32, low / len(shards), largest / len(shards))
        return jnp.repeat(jnp.exp(draws), extent[axis_at] // blocks).reshape((-1,) + (1,) * (len(extent) - axis_at - 1))

    gain = one(*shards[0])
    for cut in shards[1:]:
        gain = gain * one(*cut)
    return gain


def normal_values(stream_key, extent, width, bound, cuts=(), held_as=jnp.bfloat16):
    entries = jax.random.normal(stream_key, extent, jnp.float32) * width
    if len(cuts) > 0:
        entries = level_of(stream_key, extent, cuts, -0.22, 0.18) * entries
    return jnp.clip(entries, min=-bound, max=bound).astype(held_as)


def setup_inputs(seed: int = 0) -> dict:
    splits = jax.random.split(jax.random.key(seed), 7)
    query_in = normal_values(splits[0], (SEQ, CH), 1.0, 6.0, ((0, 16), (1, 2)))
    key_in = normal_values(splits[1], (SEQ, CH), 1.0, 6.0, ((0, 16), (1, 2)))
    value_in = normal_values(splits[2], (SEQ, CH), 1.0, 6.0, ((0, 16), (1, 2)))
    grad_out = normal_values(splits[3], (SEQ, CH), 1.0, 6.0, ((0, 16), (1, 2)))
    residue = draw_residue(jax.random.fold_in(splits[6], 71), 0)
    decay_rate = draw_decay_rate(jax.random.fold_in(splits[6], 71), 0)
    return {"query_in": query_in, "key_in": key_in, "value_in": value_in, "grad_out": grad_out, "residue": residue, "decay_rate": decay_rate}


def forward_combine(early, late):
    return (early[0] * late[0], late[0] * early[1] + late[1])

def backward_combine(right, left):
    right_a, right_b, right_g, right_p = right
    left_a, left_b, left_g, left_p = left
    return (left_a * right_a, left_a * right_b + left_b * right_a, left_a * right_g + left_g, left_a * right_p + left_b * right_g + left_p)

def channel_block(pieces):
    mixed_in, grad_mix, rates, residues = pieces
    row_count = mixed_in.shape[0]
    shape = (row_count,) + rates.shape
    factor = jnp.broadcast_to(jnp.exp(-rates), shape)
    source = jnp.broadcast_to(mixed_in[:, None, :], shape)
    _, states = lax.associative_scan(forward_combine, (factor, source), axis=0)
    conv = lax.optimization_barrier(jnp.sum(residues[None] * states, axis=1))
    target = jnp.broadcast_to(grad_mix[:, None, :], shape)
    _, _, adjoint, second = lax.associative_scan(backward_combine, (factor, factor, target, jnp.zeros(shape, jnp.float32)), axis=0, reverse=True)
    grad_conv = lax.optimization_barrier(jnp.sum(residues[None] * adjoint, axis=1))
    res_sum = lax.optimization_barrier(jnp.sum(mixed_in[:, None, :] * adjoint, axis=0))
    rate_sum = lax.optimization_barrier(jnp.sum(mixed_in[:, None, :] * second, axis=0))
    return (conv, grad_conv, res_sum, rate_sum)

def reference(query_in, key_in, value_in, grad_out, residue, decay_rate):
    mixed_in = key_in.astype(jnp.float32) * value_in.astype(jnp.float32)
    grad_mix = grad_out.astype(jnp.float32) * query_in.astype(jnp.float32)
    block_width = min(64, CH)
    block_count = CH // block_width
    mixed_t = mixed_in.reshape(SEQ, block_count, block_width).transpose(1, 0, 2)
    grad_t = grad_mix.reshape(SEQ, block_count, block_width).transpose(1, 0, 2)
    rate_t = decay_rate.reshape(M, block_count, block_width).transpose(1, 0, 2)
    res_t = residue.reshape(M, block_count, block_width).transpose(1, 0, 2)
    conv, grad_conv, res_sum, rate_sum = lax.map(channel_block, (mixed_t, grad_t, rate_t, res_t))
    conv = conv.transpose(1, 0, 2).reshape(SEQ, CH)
    grad_conv = grad_conv.transpose(1, 0, 2).reshape(SEQ, CH)
    res_sum = res_sum.transpose(1, 0, 2).reshape(M, CH)
    rate_sum = rate_sum.transpose(1, 0, 2).reshape(M, CH)
    grad_query = (grad_out.astype(jnp.float32) * conv).astype(jnp.bfloat16)
    grad_key = (grad_conv * value_in.astype(jnp.float32)).astype(jnp.bfloat16)
    grad_value = (grad_conv * key_in.astype(jnp.float32)).astype(jnp.bfloat16)
    grad_residue = res_sum / SEQ
    grad_log_rate = -decay_rate * residue * rate_sum / SEQ
    filter_norm = jnp.sqrt(jnp.sum(grad_residue * grad_residue + grad_log_rate * grad_log_rate))
    return (grad_query, grad_key, grad_value, grad_residue, grad_log_rate, filter_norm)
```

```python
import functools

import jax
import jax.numpy as jnp
from jax import lax
from jax.experimental import pallas as pl
from jax.experimental.pallas import tpu as pltpu
from jax.sharding import PartitionSpec as P

MESH = pl.DeviceIdType.MESH
LANES = 128
SUBS = 8
ROWS = 6
GROUP = 4


def local_kernel(
    query_ref, key_ref, value_ref, grad_ref, res_ref, rate_ref,
    sum_ref, span_ref, enter_ref, leave_ref, conv_ref, gconv_ref,
    mixed, gmix, tables,
):
    tile = pl.program_id(0)
    tiles = pl.num_programs(0)
    rows = mixed.shape[0]
    block = rows // SUBS
    modes = res_ref.shape[0]
    mixed[...] = key_ref[...].astype(jnp.float32) * value_ref[...].astype(jnp.float32)
    gmix[...] = grad_ref[...].astype(jnp.float32) * query_ref[...].astype(jnp.float32)
    x = [mixed[pl.ds(i, SUBS, stride=block), :] for i in range(block)]
    g = [gmix[pl.ds(i, SUBS, stride=block), :] for i in range(block)]
    rate = rate_ref[...]
    factor = jnp.exp(-rate)
    res = res_ref[...]
    power = jnp.ones_like(factor)
    taps = []
    lag_res = jnp.zeros_like(factor)
    lag_rate = jnp.zeros_like(factor)
    for j in range(block):
        taps.append(jnp.sum(res * power, axis=0, keepdims=True))
        products = x[0] * g[j]
        for i in range(1, block - j):
            products = products + x[i] * g[i + j]
        term = power * jnp.sum(products, axis=0, keepdims=True)
        lag_res = lag_res + term
        lag_rate = lag_rate + float(j) * term
        power = power * factor
    taps = [jnp.broadcast_to(h, (SUBS, LANES)) for h in taps]
    for i in range(block):
        total = taps[0] * x[i]
        for j in range(1, i + 1):
            total = total + taps[j] * x[i - j]
        conv_ref[i] = total
        total = taps[0] * g[i]
        for j in range(1, block - i):
            total = total + taps[j] * g[i + j]
        gconv_ref[i] = total
    tables[0] = factor
    tables[1] = rate
    tables[2] = lag_res
    tables[3] = lag_rate
    sub = lax.broadcasted_iota(jnp.int32, (SUBS, LANES), 0)
    before = sub.astype(jnp.float32) * float(block)
    after = (SUBS - 1 - sub).astype(jnp.float32) * float(block)

    def one_mode(m):
        f = jnp.broadcast_to(tables[0, pl.ds(m, 1), :], (SUBS, LANES))
        r = jnp.broadcast_to(tables[1, pl.ds(m, 1), :], (SUBS, LANES))
        head = x[0] * f
        head1 = head
        for i in range(1, block):
            head = (head + x[i]) * f
            head1 = head1 * f + head
        tail = g[block - 1]
        tail1 = jnp.zeros_like(tail)
        for i in range(block - 2, -1, -1):
            tail1 = (tail1 + tail) * f
            tail = tail * f + g[i]
        step = jnp.exp(r * -float(block))
        up, down, weight = head, tail, step
        for shift in (1, 2, 4):
            up = up + jnp.where(sub >= shift, weight * pltpu.roll(up, shift, 0), 0.0)
            down = down + jnp.where(
                sub < SUBS - shift, weight * pltpu.roll(down, SUBS - shift, 0), 0.0
            )
            weight = weight * weight
        enter = jnp.where(sub >= 1, pltpu.roll(up, 1, 0), 0.0)
        leave = jnp.where(sub < SUBS - 1, pltpu.roll(down, SUBS - 1, 0), 0.0)
        enter_ref[m] = enter
        leave_ref[m] = leave
        moment = jnp.exp(-r * after) * (head1 + after * head)
        gmoment = jnp.exp(-r * before) * (tail1 + before * tail)
        cross = head * leave
        cross1 = head1 * leave + enter * (tail1 + float(block) * step * leave)
        found = (
            up[SUBS - 1 :],
            down[:1],
            jnp.sum(moment, axis=0, keepdims=True),
            jnp.sum(gmoment, axis=0, keepdims=True),
            jnp.sum(cross, axis=0, keepdims=True) + tables[2, pl.ds(m, 1), :],
            jnp.sum(cross1, axis=0, keepdims=True) + tables[3, pl.ds(m, 1), :],
        )
        for at, row in enumerate(found):
            sum_ref[m, pl.ds(at * tiles + tile, 1), :] = row
        span_ref[m, pl.ds(tile, 1), :] = weight[:1]

    @pl.loop(0, modes // GROUP)
    def _(at):
        for lane in range(GROUP):
            one_mode(at * GROUP + lane)


def exchange_kernel(
    ctx, chan, positions,
    sum_ref, span_ref, res_ref, rate_ref,
    edge_ref, gres_ref, grate_ref, norm_ref,
    inbox, outbox, answer, square, send1, recv1, send2, recv2, send3, recv3,
):
    modes, width = sum_ref.shape[0], sum_ref.shape[1]
    tiles = width // ROWS
    rows = positions // ctx
    stride = ctx // modes
    me = lax.axis_index("ctx")
    mine = lax.axis_index("chan")
    mode = me // stride

    barrier = pltpu.get_barrier_semaphore()

    @pl.loop(1, ctx)
    def _(p):
        pl.semaphore_signal(
            barrier, inc=1, device_id=(lax.rem(me + p, ctx), mine), device_id_type=MESH
        )

    for p in range(1, chan):
        pl.semaphore_signal(
            barrier, inc=1, device_id=(me, lax.rem(mine + p, chan)), device_id_type=MESH
        )
    pl.semaphore_wait(barrier, ctx - 1 + chan - 1)

    def ask(m, slot, target):
        return pltpu.make_async_remote_copy(
            src_ref=sum_ref.at[m],
            dst_ref=inbox.at[slot],
            send_sem=send1.at[m],
            recv_sem=recv1.at[slot],
            device_id=(target, mine),
            device_id_type=MESH,
        )

    def reply(d, slot, target):
        return pltpu.make_async_remote_copy(
            src_ref=outbox.at[d],
            dst_ref=answer.at[slot],
            send_sem=send2.at[d],
            recv_sem=recv2.at[slot],
            device_id=(target, mine),
            device_id_type=MESH,
        )

    def owner_work():
        inbox[me] = sum_ref[mode]

        @pl.loop(1, ctx)
        def _(p):
            d = lax.rem(me + p, ctx)
            ask(mode, d, d).wait_recv()

        span = span_ref[mode]
        enter = jnp.zeros_like(span)
        for d in range(ctx):
            outbox[d, 0:tiles, :] = enter
            enter = span * enter + inbox[d, 0:tiles, :]
        leave = jnp.zeros_like(span)
        res_total = jnp.zeros_like(span)
        rate_total = jnp.zeros_like(span)
        for d in range(ctx - 1, -1, -1):
            outbox[d, tiles : 2 * tiles, :] = leave
            into = outbox[d, 0:tiles, :]
            head = inbox[d, 0:tiles, :]
            tail = inbox[d, tiles : 2 * tiles, :]
            head1 = inbox[d, 2 * tiles : 3 * tiles, :]
            tail1 = inbox[d, 3 * tiles : 4 * tiles, :]
            res_total = res_total + (inbox[d, 4 * tiles : 5 * tiles, :] + head * leave)
            rate_total = rate_total + (
                inbox[d, 5 * tiles : 6 * tiles, :]
                + head1 * leave
                + into * (tail1 + float(rows) * span * leave)
            )
            leave = span * leave + tail
        for d in range(ctx):
            outbox[d, 2 * tiles : 3 * tiles, :] = res_total
            outbox[d, 3 * tiles : 4 * tiles, :] = rate_total

        @pl.loop(1, ctx)
        def _(p):
            d = lax.rem(me + p, ctx)
            reply(d, mode, d).start()

        answer[mode] = outbox[me]

    @pl.loop(1, modes)
    def _(p):
        m = lax.rem(mode + p, modes)
        ask(m, me, m * stride).start()

    if stride == 1:
        owner_work()
    else:
        owner = lax.rem(me, stride) == 0
        pl.when(jnp.logical_not(owner))(lambda: ask(mode, me, mode * stride).start())
        pl.when(owner)(owner_work)
        pl.when(jnp.logical_not(owner))(
            lambda: reply(me, mode, mode * stride).wait_recv()
        )

    @pl.loop(1, modes)
    def _(p):
        m = lax.rem(mode + p, modes)
        reply(me, m, m * stride).wait_recv()

    edge_ref[...] = answer[:, 0 : 2 * tiles, :]
    total = jnp.zeros((1, LANES), jnp.float32)
    for t in range(tiles):
        lanes = slice(t * LANES, (t + 1) * LANES)
        grad_res = answer[:, 2 * tiles + t, :] / positions
        grad_rate = (
            -rate_ref[:, lanes] * res_ref[:, lanes] * answer[:, 3 * tiles + t, :] / positions
        )
        gres_ref[:, lanes] = grad_res
        grate_ref[:, lanes] = grad_rate
        total = total + jnp.sum(
            grad_res * grad_res + grad_rate * grad_rate, axis=0, keepdims=True
        )
    square[0] = jnp.broadcast_to(total, (SUBS, LANES))

    def partner(p):
        return pltpu.make_async_remote_copy(
            src_ref=square.at[0],
            dst_ref=square.at[p],
            send_sem=send3.at[p],
            recv_sem=recv3.at[p],
            device_id=(me, lax.rem(mine + p, chan)),
            device_id_type=MESH,
        )

    for p in range(1, chan):
        partner(p).start()
    for p in range(1, chan):
        partner(p).wait_recv()
    whole = jnp.sum(square[...], axis=0)[:1]
    norm_ref[...] = jnp.sqrt(jnp.sum(whole, axis=1, keepdims=True))

    for p in range(1, chan):
        partner(p).wait_send()

    @pl.loop(1, modes)
    def _(p):
        m = lax.rem(mode + p, modes)
        ask(m, me, m * stride).wait_send()

    def drain():
        @pl.loop(1, ctx)
        def _(p):
            d = lax.rem(me + p, ctx)
            reply(d, mode, d).wait_send()

    if stride == 1:
        drain()
    else:
        owner = lax.rem(me, stride) == 0
        pl.when(jnp.logical_not(owner))(
            lambda: ask(mode, me, mode * stride).wait_send()
        )
        pl.when(owner)(drain)


def finish_kernel(
    query_ref, key_ref, value_ref, grad_ref, res_ref, rate_ref,
    edge_ref, enter_ref, leave_ref, conv_ref, gconv_ref,
    gq_ref, gk_ref, gv_ref,
    full, gfull, tables,
):
    tile = pl.program_id(0)
    tiles = pl.num_programs(0)
    rows = full.shape[0]
    block = rows // SUBS
    modes = res_ref.shape[0]
    tables[0] = jnp.exp(-rate_ref[...])
    sub = lax.broadcasted_iota(jnp.int32, (SUBS, LANES), 0)
    before = sub.astype(jnp.float32) * float(block)
    after = (SUBS - 1 - sub).astype(jnp.float32) * float(block)

    def body(at, held):
        conv, gconv = list(held[0]), list(held[1])
        for lane in range(GROUP):
            m = at * GROUP + lane
            f = jnp.broadcast_to(tables[0, pl.ds(m, 1), :], (SUBS, LANES))
            rate = rate_ref[pl.ds(m, 1), :]
            res = res_ref[pl.ds(m, 1), :]
            into = edge_ref[m, pl.ds(tile, 1), :]
            out = edge_ref[m, pl.ds(tiles + tile, 1), :]
            z = res * (enter_ref[m] + jnp.exp(-rate * before) * into)
            y = (res * f) * (leave_ref[m] + jnp.exp(-rate * after) * out)
            for i in range(block):
                conv[i] = conv[i] + z
                gconv[block - 1 - i] = gconv[block - 1 - i] + y
                if i < block - 1:
                    z = z * f
                    y = y * f
        return tuple(conv), tuple(gconv)

    start = (
        tuple(conv_ref[i] for i in range(block)),
        tuple(gconv_ref[i] for i in range(block)),
    )
    conv, gconv = lax.fori_loop(0, modes // GROUP, body, start)
    for i in range(block):
        full[pl.ds(i, SUBS, stride=block), :] = conv[i]
        gfull[pl.ds(i, SUBS, stride=block), :] = gconv[i]
    gq_ref[...] = (grad_ref[...].astype(jnp.float32) * full[...]).astype(jnp.bfloat16)
    gk_ref[...] = (gfull[...] * value_ref[...].astype(jnp.float32)).astype(jnp.bfloat16)
    gv_ref[...] = (gfull[...] * key_ref[...].astype(jnp.float32)).astype(jnp.bfloat16)


def on_device(ctx, chan, query_in, key_in, value_in, grad_out, residue, decay_rate):
    rows, channels = query_in.shape
    modes = residue.shape[0]
    tiles = channels // LANES
    block = rows // SUBS
    f32 = jnp.float32
    data = pl.BlockSpec((rows, LANES), lambda t: (0, t))
    param = pl.BlockSpec((modes, LANES), lambda t: (0, t))
    state = pl.BlockSpec((modes, SUBS, LANES), lambda t: (0, 0, t))
    local = pl.BlockSpec((block, SUBS, LANES), lambda t: (0, 0, t))

    def whole(shape):
        return pl.BlockSpec(shape, lambda t: (0,) * len(shape))

    sums, spans, enter, leave, conv, gconv = pl.pallas_call(
        local_kernel,
        grid=(tiles,),
        in_specs=[data] * 4 + [param] * 2,
        out_specs=[
            whole((modes, ROWS * tiles, LANES)),
            whole((modes, tiles, LANES)),
            state, state, local, local,
        ],
        out_shape=[
            jax.ShapeDtypeStruct((modes, ROWS * tiles, LANES), f32),
            jax.ShapeDtypeStruct((modes, tiles, LANES), f32),
            jax.ShapeDtypeStruct((modes, SUBS, channels), f32),
            jax.ShapeDtypeStruct((modes, SUBS, channels), f32),
            jax.ShapeDtypeStruct((block, SUBS, channels), f32),
            jax.ShapeDtypeStruct((block, SUBS, channels), f32),
        ],
        scratch_shapes=[
            pltpu.VMEM((rows, LANES), f32),
            pltpu.VMEM((rows, LANES), f32),
            pltpu.VMEM((4, modes, LANES), f32),
        ],
        name="local",
    )(query_in, key_in, value_in, grad_out, residue, decay_rate)

    vmem = pl.BlockSpec(memory_space=pltpu.VMEM)
    dma = pltpu.SemaphoreType.DMA
    edges, grad_residue, grad_log_rate, norm = pl.pallas_call(
        functools.partial(exchange_kernel, ctx, chan, rows * ctx),
        in_specs=[vmem] * 4,
        out_specs=[vmem] * 4,
        out_shape=[
            jax.ShapeDtypeStruct((modes, 2 * tiles, LANES), f32),
            jax.ShapeDtypeStruct((modes, channels), f32),
            jax.ShapeDtypeStruct((modes, channels), f32),
            jax.ShapeDtypeStruct((1, 1), f32),
        ],
        scratch_shapes=[
            pltpu.VMEM((ctx, ROWS * tiles, LANES), f32),
            pltpu.VMEM((ctx, 4 * tiles, LANES), f32),
            pltpu.VMEM((modes, 4 * tiles, LANES), f32),
            pltpu.VMEM((chan, SUBS, LANES), f32),
            dma((modes,)), dma((ctx,)), dma((ctx,)), dma((modes,)),
            dma((chan,)), dma((chan,)),
        ],
        compiler_params=pltpu.CompilerParams(collective_id=0, has_side_effects=True),
        name="exchange",
    )(sums, spans, residue, decay_rate)

    grads = pl.pallas_call(
        finish_kernel,
        grid=(tiles,),
        in_specs=[data] * 4 + [param] * 2
        + [whole((modes, 2 * tiles, LANES)), state, state, local, local],
        out_specs=[data] * 3,
        out_shape=[jax.ShapeDtypeStruct((rows, channels), jnp.bfloat16)] * 3,
        scratch_shapes=[
            pltpu.VMEM((rows, LANES), f32),
            pltpu.VMEM((rows, LANES), f32),
            pltpu.VMEM((1, modes, LANES), f32),
        ],
        name="finish",
    )(
        query_in, key_in, value_in, grad_out, residue, decay_rate,
        edges, enter, leave, conv, gconv,
    )
    return (*grads, grad_residue, grad_log_rate, norm.reshape(()))


def solution(mesh):
    return jax.shard_map(
        functools.partial(on_device, mesh.shape["ctx"], mesh.shape["chan"]),
        mesh=mesh,
        in_specs=(P("ctx", "chan"),) * 4 + (P(None, "chan"),) * 2,
        out_specs=(P("ctx", "chan"),) * 3 + (P(None, "chan"),) * 2 + (P(),),
        check_vma=False,
    )
```

```python
import functools

import jax
import jax.numpy as jnp
from jax import lax
from jax.experimental import pallas as pl
from jax.experimental.pallas import tpu as pltpu
from jax.sharding import PartitionSpec as P

MESH = pl.DeviceIdType.MESH
LANES = 128
SUBS = 8
GROUP = 4


def kernel(
    ctx, chan, positions,
    query_ref, key_ref, value_ref, grad_ref, res_ref, rate_ref,
    gq_ref, gk_ref, gv_ref, gres_ref, grate_ref, norm_ref,
    mixed, gmix, factors, rates, residues, lags, enters, leaves, convs, gconvs, moments, locals_, spans,
    sums, inbox, outbox, edges, parts, partbox, total, answer, square,
    send1, recv1, send2, recv2, send3, recv3, send4, recv4, send5, recv5,
):
    modes, channels = res_ref.shape
    tiles = channels // LANES
    rows = query_ref.shape[0]
    block = rows // SUBS
    stride = ctx // modes
    me = lax.axis_index("ctx")
    mine = lax.axis_index("chan")
    mode = me // stride
    f32 = jnp.float32

    barrier = pltpu.get_barrier_semaphore()

    @pl.loop(1, ctx)
    def _(p):
        pl.semaphore_signal(
            barrier, inc=1, device_id=(lax.rem(me + p, ctx), mine), device_id_type=MESH
        )

    for p in range(1, chan):
        pl.semaphore_signal(
            barrier, inc=1, device_id=(me, lax.rem(mine + p, chan)), device_id_type=MESH
        )

    sub = lax.broadcasted_iota(jnp.int32, (SUBS, LANES), 0)
    before = sub.astype(f32) * float(block)
    after = (SUBS - 1 - sub).astype(f32) * float(block)

    def lanes_of(t):
        return pl.ds(pl.multiple_of(t * LANES, LANES), LANES)

    def blocks_of(ref, t):
        return [ref[t, pl.ds(i, SUBS, stride=block), :] for i in range(block)]

    def row_of(ref, m, t):
        return jnp.broadcast_to(ref[t, pl.ds(m, 1), :], (SUBS, LANES))

    @pl.loop(0, tiles)
    def _(t):
        lanes = lanes_of(t)
        mixed[t] = key_ref[:, lanes].astype(f32) * value_ref[:, lanes].astype(f32)
        gmix[t] = grad_ref[:, lanes].astype(f32) * query_ref[:, lanes].astype(f32)
        rates[t] = rate_ref[:, lanes]
        residues[t] = res_ref[:, lanes]
        factors[t] = jnp.exp(-rates[t])
        x = blocks_of(mixed, t)
        g = blocks_of(gmix, t)

        @pl.loop(0, modes // GROUP)
        def _(at):
            for lane in range(GROUP):
                m = at * GROUP + lane
                f = row_of(factors, m, t)
                head = x[0] * f
                tail = g[block - 1]
                for i in range(1, block):
                    head = (head + x[i]) * f
                    tail = tail * f + g[block - 1 - i]
                weight = f
                for _ in range(block.bit_length() - 1):
                    weight = weight * weight
                up, down = head, tail
                for shift in (1, 2, 4):
                    up = up + jnp.where(sub >= shift, weight * pltpu.roll(up, shift, 0), 0.0)
                    down = down + jnp.where(
                        sub < SUBS - shift, weight * pltpu.roll(down, SUBS - shift, 0), 0.0
                    )
                    weight = weight * weight
                enters[m, t] = jnp.where(sub >= 1, pltpu.roll(up, 1, 0), 0.0)
                leaves[m, t] = jnp.where(sub < SUBS - 1, pltpu.roll(down, SUBS - 1, 0), 0.0)
                sums[m, pl.ds(t, 1), :] = up[SUBS - 1 :]
                sums[m, pl.ds(tiles + t, 1), :] = down[:1]
                spans[m, pl.ds(t, 1), :] = weight[:1]

    pl.semaphore_wait(barrier, ctx - 1 + chan - 1)

    def to_owner(src, dst, sends, recvs, m, slot, target):
        return pltpu.make_async_remote_copy(
            src_ref=src.at[m],
            dst_ref=dst.at[slot],
            send_sem=sends.at[m],
            recv_sem=recvs.at[slot],
            device_id=(target, mine),
            device_id_type=MESH,
        )

    def from_owner(src, dst, sends, recvs, d, slot, target):
        return pltpu.make_async_remote_copy(
            src_ref=src.at[d] if src is outbox else src,
            dst_ref=dst.at[slot],
            send_sem=sends.at[d],
            recv_sem=recvs.at[slot],
            device_id=(target, mine),
            device_id_type=MESH,
        )

    ask = functools.partial(to_owner, sums, inbox, send1, recv1)
    reply = functools.partial(from_owner, outbox, edges, send2, recv2)
    give = functools.partial(to_owner, parts, partbox, send3, recv3)
    spread = functools.partial(from_owner, total, answer, send4, recv4)

    def if_owner(then, otherwise=None):
        if stride == 1:
            then()
            return
        owner = lax.rem(me, stride) == 0
        pl.when(owner)(then)
        if otherwise is not None:
            pl.when(jnp.logical_not(owner))(otherwise)

    def each_mode(act):
        @pl.loop(1, modes)
        def _(p):
            act(lax.rem(mode + p, modes))

    def each_peer(act):
        @pl.loop(1, ctx)
        def _(p):
            act(lax.rem(me + p, ctx))

    each_mode(lambda m: ask(m, me, m * stride).start())
    if_owner(lambda: None, lambda: ask(mode, me, mode * stride).start())

    @pl.loop(0, tiles)
    def _(t):
        lanes = lanes_of(t)
        x = blocks_of(mixed, t)
        g = blocks_of(gmix, t)
        factor = factors[t]
        res = residues[t]
        power = jnp.ones_like(factor)
        taps = []
        lag_res = jnp.zeros_like(factor)
        lag_rate = jnp.zeros_like(factor)
        for j in range(block):
            tap = jnp.sum(res * power, axis=0, keepdims=True)
            taps.append(jnp.broadcast_to(tap, (SUBS, LANES)))
            products = x[0] * g[j]
            for i in range(1, block - j):
                products = products + x[i] * g[i + j]
            term = power * jnp.sum(products, axis=0, keepdims=True)
            lag_res = lag_res + term
            lag_rate = lag_rate + float(j) * term
            power = power * factor
        for i in range(block):
            acc = taps[0] * x[i]
            for j in range(1, i + 1):
                acc = acc + taps[j] * x[i - j]
            convs[t, i] = acc
            acc = taps[0] * g[i]
            for j in range(1, block - i):
                acc = acc + taps[j] * g[i + j]
            gconvs[t, i] = acc
        lags[0] = lag_res
        lags[1] = lag_rate

        @pl.loop(0, modes // GROUP)
        def _(at):
            for lane in range(GROUP):
                m = at * GROUP + lane
                f = row_of(factors, m, t)
                head = x[0] * f
                head1 = head
                tail = g[block - 1]
                tail1 = jnp.zeros_like(tail)
                for i in range(1, block):
                    head = (head + x[i]) * f
                    head1 = head1 * f + head
                    tail1 = (tail1 + tail) * f
                    tail = tail * f + g[block - 1 - i]
                rate = rates[t, pl.ds(m, 1), :]
                enter = enters[m, t]
                leave = leaves[m, t]
                step = jnp.exp(rate * -float(block))
                moment = jnp.exp(-rate * after) * (head1 + after * head)
                gmoment = jnp.exp(-rate * before) * (tail1 + before * tail)
                cross = head * leave
                cross1 = head1 * leave + enter * (tail1 + float(block) * step * leave)
                moments[m, pl.ds(t, 1), :] = jnp.sum(moment, axis=0, keepdims=True)
                moments[m, pl.ds(tiles + t, 1), :] = jnp.sum(gmoment, axis=0, keepdims=True)
                locals_[m, pl.ds(t, 1), :] = (
                    jnp.sum(cross, axis=0, keepdims=True) + lags[0, pl.ds(m, 1), :]
                )
                locals_[m, pl.ds(tiles + t, 1), :] = (
                    jnp.sum(cross1, axis=0, keepdims=True) + lags[1, pl.ds(m, 1), :]
                )

    def owner_prefix():
        inbox[me] = sums[mode]
        each_peer(lambda d: ask(mode, d, d).wait_recv())
        span = spans[mode]
        enter = jnp.zeros_like(span)
        leave = jnp.zeros_like(span)
        for d in range(ctx):
            outbox[d, 0:tiles, :] = enter
            enter = span * enter + inbox[d, 0:tiles, :]
            back = ctx - 1 - d
            outbox[back, tiles : 2 * tiles, :] = leave
            leave = span * leave + inbox[back, tiles : 2 * tiles, :]
        each_peer(lambda d: reply(d, mode, d).start())
        edges[mode] = outbox[me]

    if_owner(owner_prefix, lambda: reply(me, mode, mode * stride).wait_recv())
    each_mode(lambda m: reply(me, m, m * stride).wait_recv())

    enter = edges[:, 0:tiles, :]
    leave = edges[:, tiles : 2 * tiles, :]
    parts[:, 0:tiles, :] = locals_[:, 0:tiles, :] + sums[:, 0:tiles, :] * leave
    parts[:, tiles : 2 * tiles, :] = (
        locals_[:, tiles : 2 * tiles, :]
        + moments[:, 0:tiles, :] * leave
        + enter * (moments[:, tiles : 2 * tiles, :] + float(rows) * spans[...] * leave)
    )
    each_mode(lambda m: give(m, me, m * stride).start())
    if_owner(lambda: None, lambda: give(mode, me, mode * stride).start())

    def finish(t):
        lanes = lanes_of(t)

        def body(at, held):
            conv, gconv = list(held[0]), list(held[1])
            for lane in range(GROUP):
                m = at * GROUP + lane
                f = row_of(factors, m, t)
                rate = rates[t, pl.ds(m, 1), :]
                res = residues[t, pl.ds(m, 1), :]
                into = edges[m, pl.ds(t, 1), :]
                out = edges[m, pl.ds(tiles + t, 1), :]
                z = res * (enters[m, t] + jnp.exp(-rate * before) * into)
                y = (res * f) * (leaves[m, t] + jnp.exp(-rate * after) * out)
                for i in range(block):
                    conv[i] = conv[i] + z
                    gconv[block - 1 - i] = gconv[block - 1 - i] + y
                    if i < block - 1:
                        z = z * f
                        y = y * f
            return tuple(conv), tuple(gconv)

        start = (
            tuple(convs[t, i] for i in range(block)),
            tuple(gconvs[t, i] for i in range(block)),
        )
        conv, gconv = lax.fori_loop(0, modes // GROUP, body, start)
        for i in range(block):
            mixed[t, pl.ds(i, SUBS, stride=block), :] = conv[i]
            gmix[t, pl.ds(i, SUBS, stride=block), :] = gconv[i]
        whole = mixed[t]
        gwhole = gmix[t]
        gq_ref[:, lanes] = (grad_ref[:, lanes].astype(f32) * whole).astype(jnp.bfloat16)
        gk_ref[:, lanes] = (gwhole * value_ref[:, lanes].astype(f32)).astype(jnp.bfloat16)
        gv_ref[:, lanes] = (gwhole * key_ref[:, lanes].astype(f32)).astype(jnp.bfloat16)

    pl.loop(0, tiles // 2)(finish)

    def owner_total():
        partbox[me] = parts[mode]
        each_peer(lambda d: give(mode, d, d).wait_recv())
        total[...] = jnp.sum(partbox[...], axis=0)
        each_peer(lambda d: spread(d, mode, d).start())
        answer[mode] = total[...]

    if_owner(owner_total)
    pl.loop(tiles // 2, tiles)(finish)
    if_owner(lambda: None, lambda: spread(me, mode, mode * stride).wait_recv())
    each_mode(lambda m: spread(me, m, m * stride).wait_recv())

    squares = jnp.zeros((1, LANES), f32)
    for t in range(tiles):
        lanes = slice(t * LANES, (t + 1) * LANES)
        grad_res = answer[:, t, :] / positions
        grad_rate = (
            -rate_ref[:, lanes] * res_ref[:, lanes] * answer[:, tiles + t, :] / positions
        )
        gres_ref[:, lanes] = grad_res
        grate_ref[:, lanes] = grad_rate
        squares = squares + jnp.sum(
            grad_res * grad_res + grad_rate * grad_rate, axis=0, keepdims=True
        )
    square[0] = jnp.broadcast_to(squares, (SUBS, LANES))

    def partner(p):
        return pltpu.make_async_remote_copy(
            src_ref=square.at[0],
            dst_ref=square.at[p],
            send_sem=send5.at[p],
            recv_sem=recv5.at[p],
            device_id=(me, lax.rem(mine + p, chan)),
            device_id_type=MESH,
        )

    for p in range(1, chan):
        partner(p).start()

    each_mode(lambda m: ask(m, me, m * stride).wait_send())
    each_mode(lambda m: give(m, me, m * stride).wait_send())

    def owner_drain():
        each_peer(lambda d: reply(d, mode, d).wait_send())
        each_peer(lambda d: spread(d, mode, d).wait_send())

    def other_drain():
        ask(mode, me, mode * stride).wait_send()
        give(mode, me, mode * stride).wait_send()

    if_owner(owner_drain, other_drain)

    for p in range(1, chan):
        partner(p).wait()
    everything = jnp.sum(square[...], axis=0)[:1]
    norm_ref[...] = jnp.sqrt(jnp.sum(everything, axis=1, keepdims=True))


def on_device(ctx, chan, query_in, key_in, value_in, grad_out, residue, decay_rate):
    rows, channels = query_in.shape
    modes = residue.shape[0]
    tiles = channels // LANES
    block = rows // SUBS
    f32 = jnp.float32
    vmem = pl.BlockSpec(memory_space=pltpu.VMEM)
    dma = pltpu.SemaphoreType.DMA

    def buffer(*shape):
        return pltpu.VMEM(shape, f32)

    *grads, norm = pl.pallas_call(
        functools.partial(kernel, ctx, chan, rows * ctx),
        in_specs=[vmem] * 6,
        out_specs=[vmem] * 6,
        out_shape=[jax.ShapeDtypeStruct((rows, channels), jnp.bfloat16)] * 3
        + [jax.ShapeDtypeStruct((modes, channels), f32)] * 2
        + [jax.ShapeDtypeStruct((1, 1), f32)],
        scratch_shapes=[
            buffer(tiles, rows, LANES),
            buffer(tiles, rows, LANES),
            buffer(tiles, modes, LANES),
            buffer(tiles, modes, LANES),
            buffer(tiles, modes, LANES),
            buffer(2, modes, LANES),
            buffer(modes, tiles, SUBS, LANES),
            buffer(modes, tiles, SUBS, LANES),
            buffer(tiles, block, SUBS, LANES),
            buffer(tiles, block, SUBS, LANES),
            buffer(modes, 2 * tiles, LANES),
            buffer(modes, 2 * tiles, LANES),
            buffer(modes, tiles, LANES),
            buffer(modes, 2 * tiles, LANES),
            buffer(ctx, 2 * tiles, LANES),
            buffer(ctx, 2 * tiles, LANES),
            buffer(modes, 2 * tiles, LANES),
            buffer(modes, 2 * tiles, LANES),
            buffer(ctx, 2 * tiles, LANES),
            buffer(2 * tiles, LANES),
            buffer(modes, 2 * tiles, LANES),
            buffer(chan, SUBS, LANES),
            dma((modes,)), dma((ctx,)), dma((ctx,)), dma((modes,)),
            dma((modes,)), dma((ctx,)), dma((ctx,)), dma((modes,)),
            dma((chan,)), dma((chan,)),
        ],
        compiler_params=pltpu.CompilerParams(
            collective_id=0, has_side_effects=True, vmem_limit_bytes=24 * 2**20
        ),
        name="hyena",
    )(query_in, key_in, value_in, grad_out, residue, decay_rate)
    return (*grads, norm.reshape(()))


def solution(mesh):
    return jax.shard_map(
        functools.partial(on_device, mesh.shape["ctx"], mesh.shape["chan"]),
        mesh=mesh,
        in_specs=(P("ctx", "chan"),) * 4 + (P(None, "chan"),) * 2,
        out_specs=(P("ctx", "chan"),) * 3 + (P(None, "chan"),) * 2 + (P(),),
        check_vma=False,
    )
```

```python
import functools

import jax
import jax.numpy as jnp
from jax import lax
from jax.experimental import pallas as pl
from jax.experimental.pallas import tpu as pltpu
from jax.sharding import PartitionSpec as P

MESH = pl.DeviceIdType.MESH
LANES = 128
SUBS = 8
GROUP = 4


def kernel(
    ctx, chan, positions,
    query_ref, key_ref, value_ref, grad_ref, res_ref, rate_ref,
    gq_ref, gk_ref, gv_ref, gres_ref, grate_ref, norm_ref,
    mixed, gmix, factors, rates, residues, lags, enters, leaves, convs, gconvs, spans,
    sums, twin, chipsum, inbox, outbox, halfedge, twinedge, edges, total, answer, square,
    send0, recv0, send1, recv1, send2, recv2, send3, recv3, send4, recv4, send5, recv5,
):
    modes, channels = res_ref.shape
    tiles = channels // LANES
    rows = query_ref.shape[0]
    block = rows // SUBS
    chips = ctx // 2
    half = modes // 2
    stride = chips // half
    me = lax.axis_index("ctx")
    mine = lax.axis_index("chan")
    chip = me // 2
    core = lax.rem(me, 2)
    sibling = 2 * chip + 1 - core
    owned = chip // stride
    mode = core * half + owned
    own_half = pl.ds(core * half, half)
    other_half = pl.ds((1 - core) * half, half)
    f32 = jnp.float32

    barrier = pltpu.get_barrier_semaphore()

    @pl.loop(1, ctx)
    def _(p):
        pl.semaphore_signal(
            barrier, inc=1, device_id=(lax.rem(me + p, ctx), mine), device_id_type=MESH
        )

    for p in range(1, chan):
        pl.semaphore_signal(
            barrier, inc=1, device_id=(me, lax.rem(mine + p, chan)), device_id_type=MESH
        )

    sub = lax.broadcasted_iota(jnp.int32, (SUBS, LANES), 0)
    before = sub.astype(f32) * float(block)
    after = (SUBS - 1 - sub).astype(f32) * float(block)

    def lanes_of(t):
        return pl.ds(pl.multiple_of(t * LANES, LANES), LANES)

    def blocks_of(ref, t):
        return [ref[t, pl.ds(i, SUBS, stride=block), :] for i in range(block)]

    def row_of(ref, m, t):
        return jnp.broadcast_to(ref[t, pl.ds(m, 1), :], (SUBS, LANES))

    @pl.loop(0, tiles)
    def _(t):
        lanes = lanes_of(t)
        mixed[t] = key_ref[:, lanes].astype(f32) * value_ref[:, lanes].astype(f32)
        gmix[t] = grad_ref[:, lanes].astype(f32) * query_ref[:, lanes].astype(f32)
        rates[t] = rate_ref[:, lanes]
        residues[t] = res_ref[:, lanes]
        factors[t] = jnp.exp(-rates[t])
        x = blocks_of(mixed, t)
        g = blocks_of(gmix, t)
        factor = factors[t]
        res = residues[t]
        power = jnp.ones_like(factor)
        taps = []
        lag_res = jnp.zeros_like(factor)
        lag_rate = jnp.zeros_like(factor)
        for j in range(block):
            tap = jnp.sum(res * power, axis=0, keepdims=True)
            taps.append(jnp.broadcast_to(tap, (SUBS, LANES)))
            products = x[0] * g[j]
            for i in range(1, block - j):
                products = products + x[i] * g[i + j]
            term = power * jnp.sum(products, axis=0, keepdims=True)
            lag_res = lag_res + term
            lag_rate = lag_rate + float(j) * term
            power = power * factor
        for i in range(block):
            acc = taps[0] * x[i]
            for j in range(1, i + 1):
                acc = acc + taps[j] * x[i - j]
            convs[t, i] = acc
            acc = taps[0] * g[i]
            for j in range(1, block - i):
                acc = acc + taps[j] * g[i + j]
            gconvs[t, i] = acc
        lags[0] = lag_res
        lags[1] = lag_rate

        @pl.loop(0, modes // GROUP)
        def _(at):
            for lane in range(GROUP):
                m = at * GROUP + lane
                f = row_of(factors, m, t)
                head = x[0] * f
                head1 = head
                tail = g[block - 1]
                tail1 = jnp.zeros_like(tail)
                for i in range(1, block):
                    head = (head + x[i]) * f
                    head1 = head1 * f + head
                    tail1 = (tail1 + tail) * f
                    tail = tail * f + g[block - 1 - i]
                rate = rates[t, pl.ds(m, 1), :]
                step = jnp.exp(rate * -float(block))
                up, down, weight = head, tail, jnp.broadcast_to(step, (SUBS, LANES))
                for shift in (1, 2, 4):
                    up = up + jnp.where(sub >= shift, weight * pltpu.roll(up, shift, 0), 0.0)
                    down = down + jnp.where(
                        sub < SUBS - shift, weight * pltpu.roll(down, SUBS - shift, 0), 0.0
                    )
                    weight = weight * weight
                enter = jnp.where(sub >= 1, pltpu.roll(up, 1, 0), 0.0)
                leave = jnp.where(sub < SUBS - 1, pltpu.roll(down, SUBS - 1, 0), 0.0)
                enters[m, t] = enter
                leaves[m, t] = leave
                moment = jnp.exp(-rate * after) * (head1 + after * head)
                gmoment = jnp.exp(-rate * before) * (tail1 + before * tail)
                cross = head * leave
                cross1 = head1 * leave + enter * (tail1 + float(block) * step * leave)
                found = (
                    up[SUBS - 1 :],
                    down[:1],
                    jnp.sum(moment, axis=0, keepdims=True),
                    jnp.sum(gmoment, axis=0, keepdims=True),
                    jnp.sum(cross, axis=0, keepdims=True) + lags[0, pl.ds(m, 1), :],
                    jnp.sum(cross1, axis=0, keepdims=True) + lags[1, pl.ds(m, 1), :],
                )
                for at_row, row in enumerate(found):
                    sums[m, pl.ds(at_row * tiles + t, 1), :] = row
                spans[m, pl.ds(t, 1), :] = weight[:1]

    pl.semaphore_wait(barrier, ctx - 1 + chan - 1)

    def remote(src, dst, send, recv, target):
        return pltpu.make_async_remote_copy(
            src_ref=src, dst_ref=dst, send_sem=send, recv_sem=recv,
            device_id=(target, mine), device_id_type=MESH,
        )

    def pair_up():
        return remote(sums.at[other_half], twin, send0, recv0, sibling)

    def ask(j, slot, at):
        return remote(
            chipsum.at[j], inbox.at[slot], send1.at[j], recv1.at[slot], 2 * at + core
        )

    def reply(h, slot):
        return remote(
            outbox.at[h], halfedge.at[slot], send2.at[h], recv2.at[slot], 2 * h + core
        )

    def pair_down():
        return remote(twinedge, edges.at[own_half], send3, recv3, sibling)

    def spread(d, slot):
        return remote(total, answer.at[slot], send4.at[d], recv4.at[slot], d)

    def if_owner(then, otherwise=None):
        if stride == 1:
            then()
            return
        owner = lax.rem(chip, stride) == 0
        pl.when(owner)(then)
        if otherwise is not None:
            pl.when(jnp.logical_not(owner))(otherwise)

    def each(count, start, act):
        @pl.loop(1, count)
        def _(p):
            act(lax.rem(start + p, count))

    def part(ref, k):
        return ref[:, k * tiles : (k + 1) * tiles, :]

    pair_up().start()
    pair_up().wait_recv()
    first = core == 0
    span = spans[own_half]

    def ordered(k):
        here = sums[own_half, k * tiles : (k + 1) * tiles, :]
        there = part(twin, k)
        return jnp.where(first, here, there), jnp.where(first, there, here)

    (xa, xb), (ga, gb), (ma, mb), (na, nb), (ra, rb), (qa, qb) = [ordered(k) for k in range(6)]
    joined = (
        span * xa + xb,
        ga + span * gb,
        span * (ma + float(rows) * xa) + mb,
        na + span * (nb + float(rows) * gb),
        ra + rb + xa * gb,
        qa + qb + ma * gb + xa * nb,
    )
    for k, found in enumerate(joined):
        chipsum[:, k * tiles : (k + 1) * tiles, :] = found

    each(half, owned, lambda j: ask(j, chip, j * stride).start())
    if_owner(lambda: None, lambda: ask(owned, chip, owned * stride).start())

    def owner_prefix():
        inbox[chip] = chipsum[owned]
        each(chips, chip, lambda h: ask(owned, h, h).wait_recv())
        span2 = spans[mode] * spans[mode]
        enter = jnp.zeros_like(span2)
        leave = jnp.zeros_like(span2)
        for h in range(chips):
            outbox[h, 0:tiles, :] = enter
            enter = span2 * enter + inbox[h, 0:tiles, :]
            back = chips - 1 - h
            outbox[back, tiles : 2 * tiles, :] = leave
            leave = span2 * leave + inbox[back, tiles : 2 * tiles, :]
        each(chips, chip, lambda h: reply(h, owned).start())
        halfedge[owned] = outbox[chip]
        enter = part(outbox, 0)
        leave = part(outbox, 1)
        res_total = part(inbox, 4) + part(inbox, 0) * leave
        rate_total = (
            part(inbox, 5)
            + part(inbox, 2) * leave
            + enter * (part(inbox, 3) + float(2 * rows) * span2 * leave)
        )
        total[0:tiles, :] = jnp.sum(res_total, axis=0)
        total[tiles : 2 * tiles, :] = jnp.sum(rate_total, axis=0)
        each(ctx, me, lambda d: spread(d, mode).start())
        answer[mode] = total[...]

    if_owner(owner_prefix, lambda: reply(chip, owned).wait_recv())
    each(half, owned, lambda j: reply(chip, j).wait_recv())

    enter = part(halfedge, 0)
    leave = part(halfedge, 1)
    enter_b = span * enter + xa
    leave_a = span * leave + gb
    edges[own_half, 0:tiles, :] = jnp.where(first, enter, enter_b)
    edges[own_half, tiles : 2 * tiles, :] = jnp.where(first, leave_a, leave)
    twinedge[:, 0:tiles, :] = jnp.where(first, enter_b, enter)
    twinedge[:, tiles : 2 * tiles, :] = jnp.where(first, leave, leave_a)
    pair_down().start()
    pair_down().wait_recv()

    def finish(t):
        lanes = lanes_of(t)

        def body(at, held):
            conv, gconv = list(held[0]), list(held[1])
            for lane in range(GROUP):
                m = at * GROUP + lane
                f = row_of(factors, m, t)
                rate = rates[t, pl.ds(m, 1), :]
                res = residues[t, pl.ds(m, 1), :]
                into = edges[m, pl.ds(t, 1), :]
                out = edges[m, pl.ds(tiles + t, 1), :]
                z = res * (enters[m, t] + jnp.exp(-rate * before) * into)
                y = (res * f) * (leaves[m, t] + jnp.exp(-rate * after) * out)
                for i in range(block):
                    conv[i] = conv[i] + z
                    gconv[block - 1 - i] = gconv[block - 1 - i] + y
                    if i < block - 1:
                        z = z * f
                        y = y * f
            return tuple(conv), tuple(gconv)

        start = (
            tuple(convs[t, i] for i in range(block)),
            tuple(gconvs[t, i] for i in range(block)),
        )
        conv, gconv = lax.fori_loop(0, modes // GROUP, body, start)
        for i in range(block):
            mixed[t, pl.ds(i, SUBS, stride=block), :] = conv[i]
            gmix[t, pl.ds(i, SUBS, stride=block), :] = gconv[i]
        whole = mixed[t]
        gwhole = gmix[t]
        gq_ref[:, lanes] = (grad_ref[:, lanes].astype(f32) * whole).astype(jnp.bfloat16)
        gk_ref[:, lanes] = (gwhole * value_ref[:, lanes].astype(f32)).astype(jnp.bfloat16)
        gv_ref[:, lanes] = (gwhole * key_ref[:, lanes].astype(f32)).astype(jnp.bfloat16)

    pl.loop(0, tiles // 2)(finish)

    if_owner(lambda: None, lambda: spread(me, mode).wait_recv())
    each(modes, mode, lambda m: spread(me, m).wait_recv())

    squares = jnp.zeros((1, LANES), f32)
    for t in range(tiles):
        lanes = slice(t * LANES, (t + 1) * LANES)
        grad_res = answer[:, t, :] / positions
        grad_rate = (
            -rate_ref[:, lanes] * res_ref[:, lanes] * answer[:, tiles + t, :] / positions
        )
        gres_ref[:, lanes] = grad_res
        grate_ref[:, lanes] = grad_rate
        squares = squares + jnp.sum(
            grad_res * grad_res + grad_rate * grad_rate, axis=0, keepdims=True
        )
    square[0] = jnp.broadcast_to(squares, (SUBS, LANES))

    def partner(p):
        return pltpu.make_async_remote_copy(
            src_ref=square.at[0],
            dst_ref=square.at[p],
            send_sem=send5.at[p],
            recv_sem=recv5.at[p],
            device_id=(me, lax.rem(mine + p, chan)),
            device_id_type=MESH,
        )

    for p in range(1, chan):
        partner(p).start()

    pl.loop(tiles // 2, tiles)(finish)

    pair_up().wait_send()
    pair_down().wait_send()
    each(half, owned, lambda j: ask(j, chip, j * stride).wait_send())

    def owner_drain():
        each(chips, chip, lambda h: reply(h, owned).wait_send())
        each(ctx, me, lambda d: spread(d, mode).wait_send())

    if_owner(owner_drain, lambda: ask(owned, chip, owned * stride).wait_send())

    for p in range(1, chan):
        partner(p).wait()
    everything = jnp.sum(square[...], axis=0)[:1]
    norm_ref[...] = jnp.sqrt(jnp.sum(everything, axis=1, keepdims=True))


def copy_kernel(*refs):
    count = len(refs) // 2
    sems = refs[-1]
    copies = [
        pltpu.make_async_copy(refs[i], refs[count + i], sems.at[i]) for i in range(count)
    ]
    for copy in copies:
        copy.start()
    for copy in copies:
        copy.wait()


def on_device(ctx, chan, query_in, key_in, value_in, grad_out, residue, decay_rate):
    rows, channels = query_in.shape
    modes = residue.shape[0]
    tiles = channels // LANES
    block = rows // SUBS
    chips = ctx // 2
    half = modes // 2
    f32 = jnp.float32
    vmem = pl.BlockSpec(memory_space=pltpu.VMEM)
    dma = pltpu.SemaphoreType.DMA

    def buffer(*shape):
        return pltpu.VMEM(shape, f32)

    shapes = (
        [jax.ShapeDtypeStruct((rows, channels), jnp.bfloat16)] * 3
        + [jax.ShapeDtypeStruct((modes, channels), f32)] * 2
        + [jax.ShapeDtypeStruct((1, 1), f32)]
    )
    found = pl.pallas_call(
        functools.partial(kernel, ctx, chan, rows * ctx),
        in_specs=[vmem] * 6,
        out_specs=[vmem] * 6,
        out_shape=shapes,
        scratch_shapes=[
            buffer(tiles, rows, LANES),
            buffer(tiles, rows, LANES),
            buffer(tiles, modes, LANES),
            buffer(tiles, modes, LANES),
            buffer(tiles, modes, LANES),
            buffer(2, modes, LANES),
            buffer(modes, tiles, SUBS, LANES),
            buffer(modes, tiles, SUBS, LANES),
            buffer(tiles, block, SUBS, LANES),
            buffer(tiles, block, SUBS, LANES),
            buffer(modes, tiles, LANES),
            buffer(modes, 6 * tiles, LANES),
            buffer(half, 6 * tiles, LANES),
            buffer(half, 6 * tiles, LANES),
            buffer(chips, 6 * tiles, LANES),
            buffer(chips, 2 * tiles, LANES),
            buffer(half, 2 * tiles, LANES),
            buffer(half, 2 * tiles, LANES),
            buffer(modes, 2 * tiles, LANES),
            buffer(2 * tiles, LANES),
            buffer(modes, 2 * tiles, LANES),
            buffer(chan, SUBS, LANES),
            dma, dma, dma((half,)), dma((chips,)), dma((chips,)), dma((half,)),
            dma, dma, dma((ctx,)), dma((modes,)), dma((chan,)), dma((chan,)),
        ],
        compiler_params=pltpu.CompilerParams(collective_id=0, has_side_effects=True),
        name="hyena",
    )(query_in, key_in, value_in, grad_out, residue, decay_rate)
    anywhere = pl.BlockSpec(memory_space=pl.ANY)
    *grads, norm = pl.pallas_call(
        copy_kernel,
        in_specs=[anywhere] * len(shapes),
        out_specs=[anywhere] * len(shapes),
        out_shape=shapes,
        scratch_shapes=[dma((len(shapes),))],
        name="place",
    )(*found)
    return (*grads, norm.reshape(()))


def solution(mesh):
    return jax.shard_map(
        functools.partial(on_device, mesh.shape["ctx"], mesh.shape["chan"]),
        mesh=mesh,
        in_specs=(P("ctx", "chan"),) * 4 + (P(None, "chan"),) * 2,
        out_specs=(P("ctx", "chan"),) * 3 + (P(None, "chan"),) * 2 + (P(),),
        check_vma=False,
    )
```

```python
import functools

import jax
import jax.numpy as jnp
from jax import lax
from jax.experimental import pallas as pl
from jax.experimental.pallas import tpu as pltpu
from jax.sharding import PartitionSpec as P

MESH = pl.DeviceIdType.MESH
LANES = 128
SUBS = 8
GROUP = 4


def kernel(
    ctx, chan, positions,
    query_ref, key_ref, value_ref, grad_ref, res_ref, rate_ref,
    gq_ref, gk_ref, gv_ref, gres_ref, grate_ref, norm_ref,
    mixed, gmix, factors, rates, residues, lags, enters, leaves, convs, gconvs, spans,
    sums, sums2, twin, twin2, chipsum, chipsum2, inbox, inbox2, outbox, halfedge, twinedge, edges, total, answer, square,
    send0, recv0, send1, recv1, send2, recv2, send3, recv3, send4, recv4, send5, recv5,
    send6, recv6, send7, recv7,
):
    modes, channels = res_ref.shape
    tiles = channels // LANES
    rows = query_ref.shape[0]
    block = rows // SUBS
    chips = ctx // 2
    half = modes // 2
    stride = chips // half
    me = lax.axis_index("ctx")
    mine = lax.axis_index("chan")
    chip = me // 2
    core = lax.rem(me, 2)
    sibling = 2 * chip + 1 - core
    owned = chip // stride
    mode = core * half + owned
    own_half = pl.ds(core * half, half)
    other_half = pl.ds((1 - core) * half, half)
    f32 = jnp.float32

    barrier = pltpu.get_barrier_semaphore()

    @pl.loop(1, ctx)
    def _(p):
        pl.semaphore_signal(
            barrier, inc=1, device_id=(lax.rem(me + p, ctx), mine), device_id_type=MESH
        )

    for p in range(1, chan):
        pl.semaphore_signal(
            barrier, inc=1, device_id=(me, lax.rem(mine + p, chan)), device_id_type=MESH
        )

    sub = lax.broadcasted_iota(jnp.int32, (SUBS, LANES), 0)
    before = sub.astype(f32) * float(block)
    after = (SUBS - 1 - sub).astype(f32) * float(block)

    def lanes_of(t):
        return pl.ds(pl.multiple_of(t * LANES, LANES), LANES)

    def blocks_of(ref, t):
        return [ref[t, pl.ds(i, SUBS, stride=block), :] for i in range(block)]

    def row_of(ref, m, t):
        return jnp.broadcast_to(ref[t, pl.ds(m, 1), :], (SUBS, LANES))

    @pl.loop(0, tiles)
    def _(t):
        lanes = lanes_of(t)
        mixed[t] = key_ref[:, lanes].astype(f32) * value_ref[:, lanes].astype(f32)
        gmix[t] = grad_ref[:, lanes].astype(f32) * query_ref[:, lanes].astype(f32)
        rates[t] = rate_ref[:, lanes]
        residues[t] = res_ref[:, lanes]
        factors[t] = jnp.exp(-rates[t])
        x = blocks_of(mixed, t)
        g = blocks_of(gmix, t)

        @pl.loop(0, modes // GROUP)
        def _(at):
            for lane in range(GROUP):
                m = at * GROUP + lane
                f = row_of(factors, m, t)
                head = x[0] * f
                tail = g[block - 1]
                for i in range(1, block):
                    head = (head + x[i]) * f
                    tail = tail * f + g[block - 1 - i]
                weight = jnp.exp(rates[t, pl.ds(m, 1), :] * -float(block))
                weight = jnp.broadcast_to(weight, (SUBS, LANES))
                up, down = head, tail
                for shift in (1, 2, 4):
                    up = up + jnp.where(sub >= shift, weight * pltpu.roll(up, shift, 0), 0.0)
                    down = down + jnp.where(
                        sub < SUBS - shift, weight * pltpu.roll(down, SUBS - shift, 0), 0.0
                    )
                    weight = weight * weight
                enters[m, t] = jnp.where(sub >= 1, pltpu.roll(up, 1, 0), 0.0)
                leaves[m, t] = jnp.where(sub < SUBS - 1, pltpu.roll(down, SUBS - 1, 0), 0.0)
                sums[m, pl.ds(t, 1), :] = up[SUBS - 1 :]
                sums[m, pl.ds(tiles + t, 1), :] = down[:1]
                spans[m, pl.ds(t, 1), :] = weight[:1]

    pl.semaphore_wait(barrier, ctx - 1 + chan - 1)

    def remote(src, dst, send, recv, target):
        return pltpu.make_async_remote_copy(
            src_ref=src, dst_ref=dst, send_sem=send, recv_sem=recv,
            device_id=(target, mine), device_id_type=MESH,
        )

    def pair_up():
        return remote(sums.at[other_half], twin, send0, recv0, sibling)

    def pair_up2():
        return remote(sums2.at[other_half], twin2, send6, recv6, sibling)

    def ask(j, slot, at):
        return remote(
            chipsum.at[j], inbox.at[slot], send1.at[j], recv1.at[slot], 2 * at + core
        )

    def ask2(j, slot, at):
        return remote(
            chipsum2.at[j], inbox2.at[slot], send7.at[j], recv7.at[slot], 2 * at + core
        )

    def reply(h, slot):
        return remote(
            outbox.at[h], halfedge.at[slot], send2.at[h], recv2.at[slot], 2 * h + core
        )

    def pair_down():
        return remote(twinedge, edges.at[own_half], send3, recv3, sibling)

    def spread(d, slot):
        return remote(total, answer.at[slot], send4.at[d], recv4.at[slot], d)

    def if_owner(then, otherwise=None):
        if stride == 1:
            then()
            return
        owner = lax.rem(chip, stride) == 0
        pl.when(owner)(then)
        if otherwise is not None:
            pl.when(jnp.logical_not(owner))(otherwise)

    def each(count, start, act):
        @pl.loop(1, count)
        def _(p):
            act(lax.rem(start + p, count))

    def part(ref, k):
        return ref[:, k * tiles : (k + 1) * tiles, :]

    pair_up().start()

    @pl.loop(0, tiles)
    def _(t):
        x = blocks_of(mixed, t)
        g = blocks_of(gmix, t)
        factor = factors[t]
        res = residues[t]
        power = jnp.ones_like(factor)
        taps = []
        lag_res = jnp.zeros_like(factor)
        lag_rate = jnp.zeros_like(factor)
        for j in range(block):
            tap = jnp.sum(res * power, axis=0, keepdims=True)
            taps.append(jnp.broadcast_to(tap, (SUBS, LANES)))
            products = x[0] * g[j]
            for i in range(1, block - j):
                products = products + x[i] * g[i + j]
            term = power * jnp.sum(products, axis=0, keepdims=True)
            lag_res = lag_res + term
            lag_rate = lag_rate + float(j) * term
            power = power * factor
        for i in range(block):
            acc = taps[0] * x[i]
            for j in range(1, i + 1):
                acc = acc + taps[j] * x[i - j]
            convs[t, i] = acc
            acc = taps[0] * g[i]
            for j in range(1, block - i):
                acc = acc + taps[j] * g[i + j]
            gconvs[t, i] = acc
        lags[0, t] = lag_res
        lags[1, t] = lag_rate

    first = core == 0
    span = spans[own_half]

    def ordered(mine_ref, twin_ref, k):
        here = mine_ref[own_half, k * tiles : (k + 1) * tiles, :]
        there = part(twin_ref, k)
        return jnp.where(first, here, there), jnp.where(first, there, here)

    pair_up().wait_recv()
    (xa, xb), (ga, gb) = [ordered(sums, twin, k) for k in range(2)]
    chipsum[:, 0:tiles, :] = span * xa + xb
    chipsum[:, tiles : 2 * tiles, :] = ga + span * gb
    each(half, owned, lambda j: ask(j, chip, j * stride).start())
    if_owner(lambda: None, lambda: ask(owned, chip, owned * stride).start())

    @pl.loop(0, tiles)
    def _(t):
        x = blocks_of(mixed, t)
        g = blocks_of(gmix, t)

        @pl.loop(0, modes // GROUP)
        def _(at):
            for lane in range(GROUP):
                m = at * GROUP + lane
                f = row_of(factors, m, t)
                head = x[0] * f
                head1 = head
                tail = g[block - 1]
                tail1 = jnp.zeros_like(tail)
                for i in range(1, block):
                    head = (head + x[i]) * f
                    head1 = head1 * f + head
                    tail1 = (tail1 + tail) * f
                    tail = tail * f + g[block - 1 - i]
                rate = rates[t, pl.ds(m, 1), :]
                step = jnp.exp(rate * -float(block))
                enter = enters[m, t]
                leave = leaves[m, t]
                moment = jnp.exp(-rate * after) * (head1 + after * head)
                gmoment = jnp.exp(-rate * before) * (tail1 + before * tail)
                cross = head * leave
                cross1 = head1 * leave + enter * (tail1 + float(block) * step * leave)
                found = (
                    jnp.sum(moment, axis=0, keepdims=True),
                    jnp.sum(gmoment, axis=0, keepdims=True),
                    jnp.sum(cross, axis=0, keepdims=True) + lags[0, t, pl.ds(m, 1), :],
                    jnp.sum(cross1, axis=0, keepdims=True) + lags[1, t, pl.ds(m, 1), :],
                )
                for at_row, row in enumerate(found):
                    sums2[m, pl.ds(at_row * tiles + t, 1), :] = row

    pair_up2().start()

    def owner_prefix():
        inbox[chip] = chipsum[owned]
        each(chips, chip, lambda h: ask(owned, h, h).wait_recv())
        span2 = spans[mode] * spans[mode]
        enter = jnp.zeros_like(span2)
        leave = jnp.zeros_like(span2)
        for h in range(chips):
            outbox[h, 0:tiles, :] = enter
            enter = span2 * enter + inbox[h, 0:tiles, :]
            back = chips - 1 - h
            outbox[back, tiles : 2 * tiles, :] = leave
            leave = span2 * leave + inbox[back, tiles : 2 * tiles, :]
        each(chips, chip, lambda h: reply(h, owned).start())
        halfedge[owned] = outbox[chip]

    if_owner(owner_prefix)

    pair_up2().wait_recv()
    (ma, mb), (na, nb), (ra, rb), (qa, qb) = [ordered(sums2, twin2, k) for k in range(4)]
    joined = (
        span * (ma + float(rows) * xa) + mb,
        na + span * (nb + float(rows) * gb),
        ra + rb + xa * gb,
        qa + qb + ma * gb + xa * nb,
    )
    for k, found in enumerate(joined):
        chipsum2[:, k * tiles : (k + 1) * tiles, :] = found
    each(half, owned, lambda j: ask2(j, chip, j * stride).start())
    if_owner(lambda: None, lambda: ask2(owned, chip, owned * stride).start())

    if_owner(lambda: None, lambda: reply(chip, owned).wait_recv())
    each(half, owned, lambda j: reply(chip, j).wait_recv())

    enter = part(halfedge, 0)
    leave = part(halfedge, 1)
    enter_b = span * enter + xa
    leave_a = span * leave + gb
    edges[own_half, 0:tiles, :] = jnp.where(first, enter, enter_b)
    edges[own_half, tiles : 2 * tiles, :] = jnp.where(first, leave_a, leave)
    twinedge[:, 0:tiles, :] = jnp.where(first, enter_b, enter)
    twinedge[:, tiles : 2 * tiles, :] = jnp.where(first, leave, leave_a)
    pair_down().start()

    def owner_totals():
        inbox2[chip] = chipsum2[owned]
        each(chips, chip, lambda h: ask2(owned, h, h).wait_recv())
        span2 = spans[mode] * spans[mode]
        enter = part(outbox, 0)
        leave = part(outbox, 1)
        res_total = part(inbox2, 2) + part(inbox, 0) * leave
        rate_total = (
            part(inbox2, 3)
            + part(inbox2, 0) * leave
            + enter * (part(inbox2, 1) + float(2 * rows) * span2 * leave)
        )
        total[0:tiles, :] = jnp.sum(res_total, axis=0)
        total[tiles : 2 * tiles, :] = jnp.sum(rate_total, axis=0)
        each(ctx, me, lambda d: spread(d, mode).start())
        answer[mode] = total[...]

    if_owner(owner_totals)
    pair_down().wait_recv()

    def finish(t):
        lanes = lanes_of(t)

        def body(at, held):
            conv, gconv = list(held[0]), list(held[1])
            for lane in range(GROUP):
                m = at * GROUP + lane
                f = row_of(factors, m, t)
                rate = rates[t, pl.ds(m, 1), :]
                res = residues[t, pl.ds(m, 1), :]
                into = edges[m, pl.ds(t, 1), :]
                out = edges[m, pl.ds(tiles + t, 1), :]
                z = res * (enters[m, t] + jnp.exp(-rate * before) * into)
                y = (res * f) * (leaves[m, t] + jnp.exp(-rate * after) * out)
                for i in range(block):
                    conv[i] = conv[i] + z
                    gconv[block - 1 - i] = gconv[block - 1 - i] + y
                    if i < block - 1:
                        z = z * f
                        y = y * f
            return tuple(conv), tuple(gconv)

        start = (
            tuple(convs[t, i] for i in range(block)),
            tuple(gconvs[t, i] for i in range(block)),
        )
        conv, gconv = lax.fori_loop(0, modes // GROUP, body, start)
        for i in range(block):
            mixed[t, pl.ds(i, SUBS, stride=block), :] = conv[i]
            gmix[t, pl.ds(i, SUBS, stride=block), :] = gconv[i]
        whole = mixed[t]
        gwhole = gmix[t]
        gq_ref[:, lanes] = (grad_ref[:, lanes].astype(f32) * whole).astype(jnp.bfloat16)
        gk_ref[:, lanes] = (gwhole * value_ref[:, lanes].astype(f32)).astype(jnp.bfloat16)
        gv_ref[:, lanes] = (gwhole * key_ref[:, lanes].astype(f32)).astype(jnp.bfloat16)

    pl.loop(0, tiles // 2)(finish)

    if_owner(lambda: None, lambda: spread(me, mode).wait_recv())
    each(modes, mode, lambda m: spread(me, m).wait_recv())

    squares = jnp.zeros((1, LANES), f32)
    for t in range(tiles):
        lanes = slice(t * LANES, (t + 1) * LANES)
        grad_res = answer[:, t, :] / positions
        grad_rate = (
            -rate_ref[:, lanes] * res_ref[:, lanes] * answer[:, tiles + t, :] / positions
        )
        gres_ref[:, lanes] = grad_res
        grate_ref[:, lanes] = grad_rate
        squares = squares + jnp.sum(
            grad_res * grad_res + grad_rate * grad_rate, axis=0, keepdims=True
        )
    square[0] = jnp.broadcast_to(squares, (SUBS, LANES))

    def partner(p):
        return pltpu.make_async_remote_copy(
            src_ref=square.at[0],
            dst_ref=square.at[p],
            send_sem=send5.at[p],
            recv_sem=recv5.at[p],
            device_id=(me, lax.rem(mine + p, chan)),
            device_id_type=MESH,
        )

    for p in range(1, chan):
        partner(p).start()

    pl.loop(tiles // 2, tiles)(finish)

    pair_up().wait_send()
    pair_down().wait_send()
    pair_up2().wait_send()
    each(half, owned, lambda j: ask(j, chip, j * stride).wait_send())
    each(half, owned, lambda j: ask2(j, chip, j * stride).wait_send())

    def owner_drain():
        each(chips, chip, lambda h: reply(h, owned).wait_send())
        each(ctx, me, lambda d: spread(d, mode).wait_send())

    def other_drain():
        ask(owned, chip, owned * stride).wait_send()
        ask2(owned, chip, owned * stride).wait_send()

    if_owner(owner_drain, other_drain)

    for p in range(1, chan):
        partner(p).wait()
    everything = jnp.sum(square[...], axis=0)[:1]
    norm_ref[...] = jnp.sqrt(jnp.sum(everything, axis=1, keepdims=True))


def copy_kernel(*refs):
    count = (len(refs) - 2) // 3
    staged = refs[2 * count : 3 * count]
    inward = [
        pltpu.make_async_copy(refs[i], staged[i], refs[-2].at[i]) for i in range(count)
    ]
    outward = [
        pltpu.make_async_copy(staged[i], refs[count + i], refs[-1].at[i]) for i in range(count)
    ]
    for copy in inward:
        copy.start()
    for i in range(count):
        inward[i].wait()
        outward[i].start()
    for copy in outward:
        copy.wait()


def on_device(ctx, chan, query_in, key_in, value_in, grad_out, residue, decay_rate):
    rows, channels = query_in.shape
    modes = residue.shape[0]
    tiles = channels // LANES
    block = rows // SUBS
    chips = ctx // 2
    half = modes // 2
    f32 = jnp.float32
    vmem = pl.BlockSpec(memory_space=pltpu.VMEM)
    dma = pltpu.SemaphoreType.DMA

    def buffer(*shape):
        return pltpu.VMEM(shape, f32)

    shapes = (
        [jax.ShapeDtypeStruct((rows, channels), jnp.bfloat16)] * 3
        + [jax.ShapeDtypeStruct((modes, channels), f32)] * 2
        + [jax.ShapeDtypeStruct((1, 1), f32)]
    )
    found = pl.pallas_call(
        functools.partial(kernel, ctx, chan, rows * ctx),
        in_specs=[vmem] * 6,
        out_specs=[vmem] * 6,
        out_shape=shapes,
        scratch_shapes=[
            buffer(tiles, rows, LANES),
            buffer(tiles, rows, LANES),
            buffer(tiles, modes, LANES),
            buffer(tiles, modes, LANES),
            buffer(tiles, modes, LANES),
            buffer(2, tiles, modes, LANES),
            buffer(modes, tiles, SUBS, LANES),
            buffer(modes, tiles, SUBS, LANES),
            buffer(tiles, block, SUBS, LANES),
            buffer(tiles, block, SUBS, LANES),
            buffer(modes, tiles, LANES),
            buffer(modes, 2 * tiles, LANES),
            buffer(modes, 4 * tiles, LANES),
            buffer(half, 2 * tiles, LANES),
            buffer(half, 4 * tiles, LANES),
            buffer(half, 2 * tiles, LANES),
            buffer(half, 4 * tiles, LANES),
            buffer(chips, 2 * tiles, LANES),
            buffer(chips, 4 * tiles, LANES),
            buffer(chips, 2 * tiles, LANES),
            buffer(half, 2 * tiles, LANES),
            buffer(half, 2 * tiles, LANES),
            buffer(modes, 2 * tiles, LANES),
            buffer(2 * tiles, LANES),
            buffer(modes, 2 * tiles, LANES),
            buffer(chan, SUBS, LANES),
            dma, dma, dma((half,)), dma((chips,)), dma((chips,)), dma((half,)),
            dma, dma, dma((ctx,)), dma((modes,)), dma((chan,)), dma((chan,)),
            dma, dma, dma((half,)), dma((chips,)),
        ],
        compiler_params=pltpu.CompilerParams(collective_id=0, has_side_effects=True),
        name="hyena",
    )(query_in, key_in, value_in, grad_out, residue, decay_rate)
    anywhere = pl.BlockSpec(memory_space=pl.ANY)
    count = len(shapes) - 1
    placed = pl.pallas_call(
        copy_kernel,
        in_specs=[anywhere] * count,
        out_specs=[anywhere] * count,
        out_shape=shapes[:count],
        scratch_shapes=[pltpu.VMEM(leaf.shape, leaf.dtype) for leaf in shapes[:count]]
        + [dma((count,)), dma((count,))],
        name="place",
    )(*found[:count])
    return (*placed, found[count].reshape(()))


def solution(mesh):
    return jax.shard_map(
        functools.partial(on_device, mesh.shape["ctx"], mesh.shape["chan"]),
        mesh=mesh,
        in_specs=(P("ctx", "chan"),) * 4 + (P(None, "chan"),) * 2,
        out_specs=(P("ctx", "chan"),) * 3 + (P(None, "chan"),) * 2 + (P(),),
        check_vma=False,
    )
```

```python
import functools

import jax
import jax.numpy as jnp
from jax import lax
from jax.experimental import pallas as pl
from jax.experimental.pallas import tpu as pltpu
from jax.sharding import PartitionSpec as P

MESH = pl.DeviceIdType.MESH
LANES = 128
SUBS = 8
GROUP = 4
UNROLL = 16


def kernel(
    ctx, chan, positions,
    query_ref, key_ref, value_ref, grad_ref, res_ref, rate_ref,
    gq_ref, gk_ref, gv_ref, gres_ref, grate_ref, norm_ref,
    mixed, gmix, factors, rates, residues, taps, lags, enters, leaves, convs, gconvs, spans,
    sums, sums2, twin, twin2, chipsum, chipsum2, inbox, inbox2, outbox, halfedge, twinedge, edges, total, answer, square,
    send0, recv0, send1, recv1, send2, recv2, send3, recv3, send4, recv4, send5, recv5,
    send6, recv6, send7, recv7,
):
    modes, channels = res_ref.shape
    tiles = channels // LANES
    rows = query_ref.shape[0]
    block = rows // SUBS
    chips = ctx // 2
    half = modes // 2
    stride = chips // half
    me = lax.axis_index("ctx")
    mine = lax.axis_index("chan")
    chip = me // 2
    core = lax.rem(me, 2)
    sibling = 2 * chip + 1 - core
    owned = chip // stride
    mode = core * half + owned
    own_half = pl.ds(core * half, half)
    other_half = pl.ds((1 - core) * half, half)
    f32 = jnp.float32

    barrier = pltpu.get_barrier_semaphore()

    @pl.loop(1, ctx, unroll=ctx <= UNROLL)
    def _(p):
        pl.semaphore_signal(
            barrier, inc=1, device_id=(lax.rem(me + p, ctx), mine), device_id_type=MESH
        )

    for p in range(1, chan):
        pl.semaphore_signal(
            barrier, inc=1, device_id=(me, lax.rem(mine + p, chan)), device_id_type=MESH
        )

    sub = lax.broadcasted_iota(jnp.int32, (SUBS, LANES), 0)
    before = sub.astype(f32) * float(block)
    after = (SUBS - 1 - sub).astype(f32) * float(block)

    def lanes_of(t):
        return pl.ds(pl.multiple_of(t * LANES, LANES), LANES)

    def blocks_of(ref, t):
        return [ref[t, pl.ds(i, SUBS, stride=block), :] for i in range(block)]

    def row_of(ref, m, t):
        return jnp.broadcast_to(ref[t, pl.ds(m, 1), :], (SUBS, LANES))

    @pl.loop(0, tiles)
    def _(t):
        lanes = lanes_of(t)
        mixed[t] = key_ref[:, lanes].astype(f32) * value_ref[:, lanes].astype(f32)
        gmix[t] = grad_ref[:, lanes].astype(f32) * query_ref[:, lanes].astype(f32)
        rates[t] = rate_ref[:, lanes]
        residues[t] = res_ref[:, lanes]
        factors[t] = jnp.exp(-rates[t])
        x = blocks_of(mixed, t)
        g = blocks_of(gmix, t)

        @pl.loop(0, modes // GROUP)
        def _(at):
            for lane in range(GROUP):
                m = at * GROUP + lane
                f = row_of(factors, m, t)
                head = x[0] * f
                tail = g[block - 1]
                for i in range(1, block):
                    head = (head + x[i]) * f
                    tail = tail * f + g[block - 1 - i]
                weight = jnp.exp(rates[t, pl.ds(m, 1), :] * -float(block))
                weight = jnp.broadcast_to(weight, (SUBS, LANES))
                up, down = head, tail
                for shift in (1, 2, 4):
                    up = up + jnp.where(sub >= shift, weight * pltpu.roll(up, shift, 0), 0.0)
                    down = down + jnp.where(
                        sub < SUBS - shift, weight * pltpu.roll(down, SUBS - shift, 0), 0.0
                    )
                    weight = weight * weight
                enters[m, t] = jnp.where(sub >= 1, pltpu.roll(up, 1, 0), 0.0)
                leaves[m, t] = jnp.where(sub < SUBS - 1, pltpu.roll(down, SUBS - 1, 0), 0.0)
                sums[m, pl.ds(t, 1), :] = up[SUBS - 1 :]
                sums[m, pl.ds(tiles + t, 1), :] = down[:1]
                spans[m, pl.ds(t, 1), :] = weight[:1]

    pl.semaphore_wait(barrier, ctx - 1 + chan - 1)

    def remote(src, dst, send, recv, target):
        return pltpu.make_async_remote_copy(
            src_ref=src, dst_ref=dst, send_sem=send, recv_sem=recv,
            device_id=(target, mine), device_id_type=MESH,
        )

    def pair_up():
        return remote(sums.at[other_half], twin, send0, recv0, sibling)

    def pair_up2():
        return remote(sums2.at[other_half], twin2, send6, recv6, sibling)

    def ask(j, slot, at):
        return remote(
            chipsum.at[j], inbox.at[slot], send1.at[j], recv1.at[slot], 2 * at + core
        )

    def ask2(j, slot, at):
        return remote(
            chipsum2.at[j], inbox2.at[slot], send7.at[j], recv7.at[slot], 2 * at + core
        )

    def reply(h, slot):
        return remote(
            outbox.at[h], halfedge.at[slot], send2.at[h], recv2.at[slot], 2 * h + core
        )

    def pair_down():
        return remote(twinedge, edges.at[own_half], send3, recv3, sibling)

    def spread(d, slot):
        return remote(total, answer.at[slot], send4.at[d], recv4.at[slot], d)

    def if_owner(then, otherwise=None):
        if stride == 1:
            then()
            return
        owner = lax.rem(chip, stride) == 0
        pl.when(owner)(then)
        if otherwise is not None:
            pl.when(jnp.logical_not(owner))(otherwise)

    def each(count, start, act):
        @pl.loop(1, count, unroll=count <= UNROLL)
        def _(p):
            act(lax.rem(start + p, count))

    def part(ref, k):
        return ref[:, k * tiles : (k + 1) * tiles, :]

    pair_up().start()

    @pl.loop(0, tiles)
    def _(t):
        x = blocks_of(mixed, t)
        g = blocks_of(gmix, t)
        factor = factors[t]
        res = residues[t]
        power = jnp.ones_like(factor)
        lag_res = jnp.zeros_like(factor)
        lag_rate = jnp.zeros_like(factor)
        for j in range(block):
            tap = jnp.sum(res * power, axis=0, keepdims=True)
            taps[t, j] = jnp.broadcast_to(tap, (SUBS, LANES))
            products = x[0] * g[j]
            for i in range(1, block - j):
                products = products + x[i] * g[i + j]
            term = power * jnp.sum(products, axis=0, keepdims=True)
            lag_res = lag_res + term
            lag_rate = lag_rate + float(j) * term
            power = power * factor
        lags[0, t] = lag_res
        lags[1, t] = lag_rate

    first = core == 0
    span = spans[own_half]

    def ordered(mine_ref, twin_ref, k):
        here = mine_ref[own_half, k * tiles : (k + 1) * tiles, :]
        there = part(twin_ref, k)
        return jnp.where(first, here, there), jnp.where(first, there, here)

    pair_up().wait_recv()
    (xa, xb), (ga, gb) = [ordered(sums, twin, k) for k in range(2)]
    chipsum[:, 0:tiles, :] = span * xa + xb
    chipsum[:, tiles : 2 * tiles, :] = ga + span * gb
    each(half, owned, lambda j: ask(j, chip, j * stride).start())
    if_owner(lambda: None, lambda: ask(owned, chip, owned * stride).start())

    @pl.loop(0, tiles)
    def _(t):
        x = blocks_of(mixed, t)
        g = blocks_of(gmix, t)

        @pl.loop(0, modes // GROUP)
        def _(at):
            for lane in range(GROUP):
                m = at * GROUP + lane
                f = row_of(factors, m, t)
                head = x[0] * f
                head1 = head
                tail = g[block - 1]
                tail1 = jnp.zeros_like(tail)
                for i in range(1, block):
                    head = (head + x[i]) * f
                    head1 = head1 * f + head
                    tail1 = (tail1 + tail) * f
                    tail = tail * f + g[block - 1 - i]
                rate = rates[t, pl.ds(m, 1), :]
                step = jnp.exp(rate * -float(block))
                enter = enters[m, t]
                leave = leaves[m, t]
                moment = jnp.exp(-rate * after) * (head1 + after * head)
                gmoment = jnp.exp(-rate * before) * (tail1 + before * tail)
                cross = head * leave
                cross1 = head1 * leave + enter * (tail1 + float(block) * step * leave)
                found = (
                    jnp.sum(moment, axis=0, keepdims=True),
                    jnp.sum(gmoment, axis=0, keepdims=True),
                    jnp.sum(cross, axis=0, keepdims=True) + lags[0, t, pl.ds(m, 1), :],
                    jnp.sum(cross1, axis=0, keepdims=True) + lags[1, t, pl.ds(m, 1), :],
                )
                for at_row, row in enumerate(found):
                    sums2[m, pl.ds(at_row * tiles + t, 1), :] = row

    pair_up2().start()

    def owner_prefix():
        inbox[chip] = chipsum[owned]
        each(chips, chip, lambda h: ask(owned, h, h).wait_recv())
        span2 = spans[mode] * spans[mode]
        enter = jnp.zeros_like(span2)
        leave = jnp.zeros_like(span2)
        for h in range(chips):
            outbox[h, 0:tiles, :] = enter
            enter = span2 * enter + inbox[h, 0:tiles, :]
            back = chips - 1 - h
            outbox[back, tiles : 2 * tiles, :] = leave
            leave = span2 * leave + inbox[back, tiles : 2 * tiles, :]
        each(chips, chip, lambda h: reply(h, owned).start())
        halfedge[owned] = outbox[chip]

    if_owner(owner_prefix)

    pair_up2().wait_recv()
    (ma, mb), (na, nb), (ra, rb), (qa, qb) = [ordered(sums2, twin2, k) for k in range(4)]
    joined = (
        span * (ma + float(rows) * xa) + mb,
        na + span * (nb + float(rows) * gb),
        ra + rb + xa * gb,
        qa + qb + ma * gb + xa * nb,
    )
    for k, found in enumerate(joined):
        chipsum2[:, k * tiles : (k + 1) * tiles, :] = found
    each(half, owned, lambda j: ask2(j, chip, j * stride).start())
    if_owner(lambda: None, lambda: ask2(owned, chip, owned * stride).start())

    @pl.loop(0, tiles)
    def _(t):
        x = blocks_of(mixed, t)
        g = blocks_of(gmix, t)
        h = [taps[t, j] for j in range(block)]
        for i in range(block):
            acc = h[0] * x[i]
            for j in range(1, i + 1):
                acc = acc + h[j] * x[i - j]
            convs[t, i] = acc
            acc = h[0] * g[i]
            for j in range(1, block - i):
                acc = acc + h[j] * g[i + j]
            gconvs[t, i] = acc

    if_owner(lambda: None, lambda: reply(chip, owned).wait_recv())
    each(half, owned, lambda j: reply(chip, j).wait_recv())

    enter = part(halfedge, 0)
    leave = part(halfedge, 1)
    enter_b = span * enter + xa
    leave_a = span * leave + gb
    edges[own_half, 0:tiles, :] = jnp.where(first, enter, enter_b)
    edges[own_half, tiles : 2 * tiles, :] = jnp.where(first, leave_a, leave)
    twinedge[:, 0:tiles, :] = jnp.where(first, enter_b, enter)
    twinedge[:, tiles : 2 * tiles, :] = jnp.where(first, leave, leave_a)
    pair_down().start()

    def owner_totals():
        inbox2[chip] = chipsum2[owned]
        each(chips, chip, lambda h: ask2(owned, h, h).wait_recv())
        span2 = spans[mode] * spans[mode]
        enter = part(outbox, 0)
        leave = part(outbox, 1)
        res_total = part(inbox2, 2) + part(inbox, 0) * leave
        rate_total = (
            part(inbox2, 3)
            + part(inbox2, 0) * leave
            + enter * (part(inbox2, 1) + float(2 * rows) * span2 * leave)
        )
        total[0:tiles, :] = jnp.sum(res_total, axis=0)
        total[tiles : 2 * tiles, :] = jnp.sum(rate_total, axis=0)
        each(ctx, me, lambda d: spread(d, mode).start())
        answer[mode] = total[...]

    if_owner(owner_totals)
    pair_down().wait_recv()

    def finish(t):
        lanes = lanes_of(t)

        def body(at, held):
            conv, gconv = list(held[0]), list(held[1])
            for lane in range(GROUP):
                m = at * GROUP + lane
                f = row_of(factors, m, t)
                rate = rates[t, pl.ds(m, 1), :]
                res = residues[t, pl.ds(m, 1), :]
                into = edges[m, pl.ds(t, 1), :]
                out = edges[m, pl.ds(tiles + t, 1), :]
                z = res * (enters[m, t] + jnp.exp(-rate * before) * into)
                y = (res * f) * (leaves[m, t] + jnp.exp(-rate * after) * out)
                for i in range(block):
                    conv[i] = conv[i] + z
                    gconv[block - 1 - i] = gconv[block - 1 - i] + y
                    if i < block - 1:
                        z = z * f
                        y = y * f
            return tuple(conv), tuple(gconv)

        start = (
            tuple(convs[t, i] for i in range(block)),
            tuple(gconvs[t, i] for i in range(block)),
        )
        conv, gconv = lax.fori_loop(0, modes // GROUP, body, start)
        for i in range(block):
            mixed[t, pl.ds(i, SUBS, stride=block), :] = conv[i]
            gmix[t, pl.ds(i, SUBS, stride=block), :] = gconv[i]
        whole = mixed[t]
        gwhole = gmix[t]
        gq_ref[:, lanes] = (grad_ref[:, lanes].astype(f32) * whole).astype(jnp.bfloat16)
        gk_ref[:, lanes] = (gwhole * value_ref[:, lanes].astype(f32)).astype(jnp.bfloat16)
        gv_ref[:, lanes] = (gwhole * key_ref[:, lanes].astype(f32)).astype(jnp.bfloat16)

    pl.loop(0, tiles // 2)(finish)

    if_owner(lambda: None, lambda: spread(me, mode).wait_recv())
    each(modes, mode, lambda m: spread(me, m).wait_recv())

    squares = jnp.zeros((1, LANES), f32)
    for t in range(tiles):
        lanes = slice(t * LANES, (t + 1) * LANES)
        grad_res = answer[:, t, :] / positions
        grad_rate = (
            -rate_ref[:, lanes] * res_ref[:, lanes] * answer[:, tiles + t, :] / positions
        )
        gres_ref[:, lanes] = grad_res
        grate_ref[:, lanes] = grad_rate
        squares = squares + jnp.sum(
            grad_res * grad_res + grad_rate * grad_rate, axis=0, keepdims=True
        )
    square[0] = jnp.broadcast_to(squares, (SUBS, LANES))

    def partner(p):
        return pltpu.make_async_remote_copy(
            src_ref=square.at[0],
            dst_ref=square.at[p],
            send_sem=send5.at[p],
            recv_sem=recv5.at[p],
            device_id=(me, lax.rem(mine + p, chan)),
            device_id_type=MESH,
        )

    for p in range(1, chan):
        partner(p).start()

    pl.loop(tiles // 2, tiles)(finish)

    pair_up().wait_send()
    pair_down().wait_send()
    pair_up2().wait_send()
    each(half, owned, lambda j: ask(j, chip, j * stride).wait_send())
    each(half, owned, lambda j: ask2(j, chip, j * stride).wait_send())

    def owner_drain():
        each(chips, chip, lambda h: reply(h, owned).wait_send())
        each(ctx, me, lambda d: spread(d, mode).wait_send())

    def other_drain():
        ask(owned, chip, owned * stride).wait_send()
        ask2(owned, chip, owned * stride).wait_send()

    if_owner(owner_drain, other_drain)

    for p in range(1, chan):
        partner(p).wait()
    everything = jnp.sum(square[...], axis=0)[:1]
    norm_ref[...] = jnp.sqrt(jnp.sum(everything, axis=1, keepdims=True))


def copy_kernel(*refs):
    count = (len(refs) - 2) // 3
    staged = refs[2 * count : 3 * count]
    inward = [
        pltpu.make_async_copy(refs[i], staged[i], refs[-2].at[i]) for i in range(count)
    ]
    outward = [
        pltpu.make_async_copy(staged[i], refs[count + i], refs[-1].at[i]) for i in range(count)
    ]
    for copy in inward:
        copy.start()
    for i in range(count):
        inward[i].wait()
        outward[i].start()
    for copy in outward:
        copy.wait()


def on_device(ctx, chan, query_in, key_in, value_in, grad_out, residue, decay_rate):
    rows, channels = query_in.shape
    modes = residue.shape[0]
    tiles = channels // LANES
    block = rows // SUBS
    chips = ctx // 2
    half = modes // 2
    f32 = jnp.float32
    vmem = pl.BlockSpec(memory_space=pltpu.VMEM)
    dma = pltpu.SemaphoreType.DMA

    def buffer(*shape):
        return pltpu.VMEM(shape, f32)

    shapes = (
        [jax.ShapeDtypeStruct((rows, channels), jnp.bfloat16)] * 3
        + [jax.ShapeDtypeStruct((modes, channels), f32)] * 2
        + [jax.ShapeDtypeStruct((1, 1), f32)]
    )
    found = pl.pallas_call(
        functools.partial(kernel, ctx, chan, rows * ctx),
        in_specs=[vmem] * 6,
        out_specs=[vmem] * 6,
        out_shape=shapes,
        scratch_shapes=[
            buffer(tiles, rows, LANES),
            buffer(tiles, rows, LANES),
            buffer(tiles, modes, LANES),
            buffer(tiles, modes, LANES),
            buffer(tiles, modes, LANES),
            buffer(tiles, block, SUBS, LANES),
            buffer(2, tiles, modes, LANES),
            buffer(modes, tiles, SUBS, LANES),
            buffer(modes, tiles, SUBS, LANES),
            buffer(tiles, block, SUBS, LANES),
            buffer(tiles, block, SUBS, LANES),
            buffer(modes, tiles, LANES),
            buffer(modes, 2 * tiles, LANES),
            buffer(modes, 4 * tiles, LANES),
            buffer(half, 2 * tiles, LANES),
            buffer(half, 4 * tiles, LANES),
            buffer(half, 2 * tiles, LANES),
            buffer(half, 4 * tiles, LANES),
            buffer(chips, 2 * tiles, LANES),
            buffer(chips, 4 * tiles, LANES),
            buffer(chips, 2 * tiles, LANES),
            buffer(half, 2 * tiles, LANES),
            buffer(half, 2 * tiles, LANES),
            buffer(modes, 2 * tiles, LANES),
            buffer(2 * tiles, LANES),
            buffer(modes, 2 * tiles, LANES),
            buffer(chan, SUBS, LANES),
            dma, dma, dma((half,)), dma((chips,)), dma((chips,)), dma((half,)),
            dma, dma, dma((ctx,)), dma((modes,)), dma((chan,)), dma((chan,)),
            dma, dma, dma((half,)), dma((chips,)),
        ],
        compiler_params=pltpu.CompilerParams(collective_id=0, has_side_effects=True),
        name="hyena",
    )(query_in, key_in, value_in, grad_out, residue, decay_rate)
    anywhere = pl.BlockSpec(memory_space=pl.ANY)
    count = len(shapes) - 1
    placed = pl.pallas_call(
        copy_kernel,
        in_specs=[anywhere] * count,
        out_specs=[anywhere] * count,
        out_shape=shapes[:count],
        scratch_shapes=[pltpu.VMEM(leaf.shape, leaf.dtype) for leaf in shapes[:count]]
        + [dma((count,)), dma((count,))],
        name="place",
    )(*found[:count])
    return (*placed, found[count].reshape(()))


def solution(mesh):
    return jax.shard_map(
        functools.partial(on_device, mesh.shape["ctx"], mesh.shape["chan"]),
        mesh=mesh,
        in_specs=(P("ctx", "chan"),) * 4 + (P(None, "chan"),) * 2,
        out_specs=(P("ctx", "chan"),) * 3 + (P(None, "chan"),) * 2 + (P(),),
        check_vma=False,
    )
```

```python
import functools

import jax
import jax.numpy as jnp
from jax import lax
from jax.experimental import pallas as pl
from jax.experimental.pallas import tpu as pltpu
from jax.sharding import PartitionSpec as P

MESH = pl.DeviceIdType.MESH
LANES = 128
SUBS = 8
GROUP = 4
UNROLL = 16


def kernel(
    ctx, chan, positions,
    query_ref, key_ref, value_ref, grad_ref, res_ref, rate_ref,
    gq_ref, gk_ref, gv_ref, gres_ref, grate_ref, norm_ref,
    mixed, gmix, factors, rates, residues, taps, lags, enters, leaves, convs, gconvs, spans,
    sums, twin, chipsum, inbox, outbox, heard, edges, total, answer, square,
    send0, recv0, send1, recv1, send2, recv2, send3, recv3, send4, recv4, send5, recv5,
):
    modes, channels = res_ref.shape
    tiles = channels // LANES
    rows = query_ref.shape[0]
    block = rows // SUBS
    chips = ctx // 2
    half = modes // 2
    stride = chips // half
    me = lax.axis_index("ctx")
    mine = lax.axis_index("chan")
    chip = me // 2
    core = lax.rem(me, 2)
    sibling = 2 * chip + 1 - core
    owned = chip // stride
    mode = core * half + owned
    own_half = pl.ds(core * half, half)
    other_half = pl.ds((1 - core) * half, half)
    f32 = jnp.float32

    barrier = pltpu.get_barrier_semaphore()

    @pl.loop(1, ctx, unroll=ctx <= UNROLL)
    def _(p):
        pl.semaphore_signal(
            barrier, inc=1, device_id=(lax.rem(me + p, ctx), mine), device_id_type=MESH
        )

    for p in range(1, chan):
        pl.semaphore_signal(
            barrier, inc=1, device_id=(me, lax.rem(mine + p, chan)), device_id_type=MESH
        )

    sub = lax.broadcasted_iota(jnp.int32, (SUBS, LANES), 0)
    before = sub.astype(f32) * float(block)
    after = (SUBS - 1 - sub).astype(f32) * float(block)

    def lanes_of(t):
        return pl.ds(pl.multiple_of(t * LANES, LANES), LANES)

    def blocks_of(ref, t):
        return [ref[t, pl.ds(i, SUBS, stride=block), :] for i in range(block)]

    def row_of(ref, m, t):
        return jnp.broadcast_to(ref[t, pl.ds(m, 1), :], (SUBS, LANES))

    @pl.loop(0, tiles)
    def _(t):
        lanes = lanes_of(t)
        mixed[t] = key_ref[:, lanes].astype(f32) * value_ref[:, lanes].astype(f32)
        gmix[t] = grad_ref[:, lanes].astype(f32) * query_ref[:, lanes].astype(f32)
        rates[t] = rate_ref[:, lanes]
        residues[t] = res_ref[:, lanes]
        factors[t] = jnp.exp(-rates[t])
        x = blocks_of(mixed, t)
        g = blocks_of(gmix, t)
        factor = factors[t]
        res = residues[t]
        power = jnp.ones_like(factor)
        lag_res = jnp.zeros_like(factor)
        lag_rate = jnp.zeros_like(factor)
        for j in range(block):
            tap = jnp.sum(res * power, axis=0, keepdims=True)
            taps[t, j] = jnp.broadcast_to(tap, (SUBS, LANES))
            products = x[0] * g[j]
            for i in range(1, block - j):
                products = products + x[i] * g[i + j]
            term = power * jnp.sum(products, axis=0, keepdims=True)
            lag_res = lag_res + term
            lag_rate = lag_rate + float(j) * term
            power = power * factor
        lags[0, t] = lag_res
        lags[1, t] = lag_rate

        @pl.loop(0, modes // GROUP)
        def _(at):
            for lane in range(GROUP):
                m = at * GROUP + lane
                f = row_of(factors, m, t)
                head = x[0] * f
                head1 = head
                tail = g[block - 1]
                tail1 = jnp.zeros_like(tail)
                for i in range(1, block):
                    head = (head + x[i]) * f
                    head1 = head1 * f + head
                    tail1 = (tail1 + tail) * f
                    tail = tail * f + g[block - 1 - i]
                rate = rates[t, pl.ds(m, 1), :]
                step = jnp.exp(rate * -float(block))
                up, down, weight = head, tail, jnp.broadcast_to(step, (SUBS, LANES))
                for shift in (1, 2, 4):
                    up = up + jnp.where(sub >= shift, weight * pltpu.roll(up, shift, 0), 0.0)
                    down = down + jnp.where(
                        sub < SUBS - shift, weight * pltpu.roll(down, SUBS - shift, 0), 0.0
                    )
                    weight = weight * weight
                enter = jnp.where(sub >= 1, pltpu.roll(up, 1, 0), 0.0)
                leave = jnp.where(sub < SUBS - 1, pltpu.roll(down, SUBS - 1, 0), 0.0)
                enters[m, t] = enter
                leaves[m, t] = leave
                moment = jnp.exp(-rate * after) * (head1 + after * head)
                gmoment = jnp.exp(-rate * before) * (tail1 + before * tail)
                cross = head * leave
                cross1 = head1 * leave + enter * (tail1 + float(block) * step * leave)
                found = (
                    up[SUBS - 1 :],
                    down[:1],
                    jnp.sum(moment, axis=0, keepdims=True),
                    jnp.sum(gmoment, axis=0, keepdims=True),
                    jnp.sum(cross, axis=0, keepdims=True) + lags[0, t, pl.ds(m, 1), :],
                    jnp.sum(cross1, axis=0, keepdims=True) + lags[1, t, pl.ds(m, 1), :],
                )
                for at_row, row in enumerate(found):
                    sums[m, pl.ds(at_row * tiles + t, 1), :] = row
                spans[m, pl.ds(t, 1), :] = weight[:1]

    pl.semaphore_wait(barrier, ctx - 1 + chan - 1)

    def remote(src, dst, send, recv, target):
        return pltpu.make_async_remote_copy(
            src_ref=src, dst_ref=dst, send_sem=send, recv_sem=recv,
            device_id=(target, mine), device_id_type=MESH,
        )

    def pair_up():
        return remote(sums.at[other_half], twin.at[other_half], send0, recv0, sibling)

    def pair_rest():
        return remote(sums.at[own_half], twin.at[own_half], send3, recv3, sibling)

    def ask(j, slot, at):
        return remote(
            chipsum.at[j], inbox.at[slot], send1.at[j], recv1.at[slot], 2 * at + core
        )

    def reply(d, slot):
        return remote(outbox.at[d // 2], heard.at[slot], send2.at[d], recv2.at[slot], d)

    def spread(d, slot):
        return remote(total, answer.at[slot], send4.at[d], recv4.at[slot], d)

    def if_owner(then, otherwise=None):
        if stride == 1:
            then()
            return
        owner = lax.rem(chip, stride) == 0
        pl.when(owner)(then)
        if otherwise is not None:
            pl.when(jnp.logical_not(owner))(otherwise)

    def each(count, start, act):
        @pl.loop(1, count, unroll=count <= UNROLL)
        def _(p):
            act(lax.rem(start + p, count))

    def part(ref, k):
        return ref[:, k * tiles : (k + 1) * tiles, :]

    pair_up().start()
    pair_rest().start()
    first = core == 0
    span = spans[own_half]

    def ordered(k):
        here = sums[own_half, k * tiles : (k + 1) * tiles, :]
        there = twin[own_half, k * tiles : (k + 1) * tiles, :]
        return jnp.where(first, here, there), jnp.where(first, there, here)

    pair_up().wait_recv()
    (xa, xb), (ga, gb), (ma, mb), (na, nb), (ra, rb), (qa, qb) = [ordered(k) for k in range(6)]
    joined = (
        span * xa + xb,
        ga + span * gb,
        span * (ma + float(rows) * xa) + mb,
        na + span * (nb + float(rows) * gb),
        ra + rb + xa * gb,
        qa + qb + ma * gb + xa * nb,
    )
    for k, found in enumerate(joined):
        chipsum[:, k * tiles : (k + 1) * tiles, :] = found
    each(half, owned, lambda j: ask(j, chip, j * stride).start())
    if_owner(lambda: None, lambda: ask(owned, chip, owned * stride).start())

    @pl.loop(0, tiles)
    def _(t):
        x = blocks_of(mixed, t)
        g = blocks_of(gmix, t)
        h = [taps[t, j] for j in range(block)]
        for i in range(block):
            acc = h[0] * x[i]
            for j in range(1, i + 1):
                acc = acc + h[j] * x[i - j]
            convs[t, i] = acc
            acc = h[0] * g[i]
            for j in range(1, block - i):
                acc = acc + h[j] * g[i + j]
            gconvs[t, i] = acc

    def owner_work():
        inbox[chip] = chipsum[owned]
        each(chips, chip, lambda h: ask(owned, h, h).wait_recv())
        span2 = spans[mode] * spans[mode]
        enter = jnp.zeros_like(span2)
        leave = jnp.zeros_like(span2)
        for h in range(chips):
            outbox[h, 0:tiles, :] = enter
            enter = span2 * enter + inbox[h, 0:tiles, :]
            back = chips - 1 - h
            outbox[back, tiles : 2 * tiles, :] = leave
            leave = span2 * leave + inbox[back, tiles : 2 * tiles, :]
        each(ctx, me, lambda d: reply(d, mode).start())
        heard[mode] = outbox[chip]
        enter = part(outbox, 0)
        leave = part(outbox, 1)
        res_total = part(inbox, 4) + part(inbox, 0) * leave
        rate_total = (
            part(inbox, 5)
            + part(inbox, 2) * leave
            + enter * (part(inbox, 3) + float(2 * rows) * span2 * leave)
        )
        total[0:tiles, :] = jnp.sum(res_total, axis=0)
        total[tiles : 2 * tiles, :] = jnp.sum(rate_total, axis=0)
        each(ctx, me, lambda d: spread(d, mode).start())
        answer[mode] = total[...]

    if_owner(owner_work, lambda: reply(me, mode).wait_recv())
    pair_rest().wait_recv()
    each(modes, mode, lambda m: reply(me, m).wait_recv())

    enter = part(heard, 0)
    leave = part(heard, 1)
    edges[:, 0:tiles, :] = jnp.where(first, enter, spans[...] * enter + part(twin, 0))
    edges[:, tiles : 2 * tiles, :] = jnp.where(first, spans[...] * leave + part(twin, 1), leave)

    def finish(t):
        lanes = lanes_of(t)

        def body(at, held):
            conv, gconv = list(held[0]), list(held[1])
            for lane in range(GROUP):
                m = at * GROUP + lane
                f = row_of(factors, m, t)
                rate = rates[t, pl.ds(m, 1), :]
                res = residues[t, pl.ds(m, 1), :]
                into = edges[m, pl.ds(t, 1), :]
                out = edges[m, pl.ds(tiles + t, 1), :]
                z = res * (enters[m, t] + jnp.exp(-rate * before) * into)
                y = (res * f) * (leaves[m, t] + jnp.exp(-rate * after) * out)
                for i in range(block):
                    conv[i] = conv[i] + z
                    gconv[block - 1 - i] = gconv[block - 1 - i] + y
                    if i < block - 1:
                        z = z * f
                        y = y * f
            return tuple(conv), tuple(gconv)

        start = (
            tuple(convs[t, i] for i in range(block)),
            tuple(gconvs[t, i] for i in range(block)),
        )
        conv, gconv = lax.fori_loop(0, modes // GROUP, body, start)
        for i in range(block):
            mixed[t, pl.ds(i, SUBS, stride=block), :] = conv[i]
            gmix[t, pl.ds(i, SUBS, stride=block), :] = gconv[i]
        whole = mixed[t]
        gwhole = gmix[t]
        gq_ref[:, lanes] = (grad_ref[:, lanes].astype(f32) * whole).astype(jnp.bfloat16)
        gk_ref[:, lanes] = (gwhole * value_ref[:, lanes].astype(f32)).astype(jnp.bfloat16)
        gv_ref[:, lanes] = (gwhole * key_ref[:, lanes].astype(f32)).astype(jnp.bfloat16)

    pl.loop(0, tiles // 4)(finish)

    if_owner(lambda: None, lambda: spread(me, mode).wait_recv())
    each(modes, mode, lambda m: spread(me, m).wait_recv())

    squares = jnp.zeros((1, LANES), f32)
    for t in range(tiles):
        lanes = slice(t * LANES, (t + 1) * LANES)
        grad_res = answer[:, t, :] / positions
        grad_rate = (
            -rate_ref[:, lanes] * res_ref[:, lanes] * answer[:, tiles + t, :] / positions
        )
        gres_ref[:, lanes] = grad_res
        grate_ref[:, lanes] = grad_rate
        squares = squares + jnp.sum(
            grad_res * grad_res + grad_rate * grad_rate, axis=0, keepdims=True
        )
    square[0] = jnp.broadcast_to(squares, (SUBS, LANES))

    def partner(p):
        return pltpu.make_async_remote_copy(
            src_ref=square.at[0],
            dst_ref=square.at[p],
            send_sem=send5.at[p],
            recv_sem=recv5.at[p],
            device_id=(me, lax.rem(mine + p, chan)),
            device_id_type=MESH,
        )

    for p in range(1, chan):
        partner(p).start()

    pl.loop(tiles // 4, tiles)(finish)

    pair_up().wait_send()
    pair_rest().wait_send()
    each(half, owned, lambda j: ask(j, chip, j * stride).wait_send())

    def owner_drain():
        each(ctx, me, lambda d: reply(d, mode).wait_send())
        each(ctx, me, lambda d: spread(d, mode).wait_send())

    def other_drain():
        ask(owned, chip, owned * stride).wait_send()

    if_owner(owner_drain, other_drain)

    for p in range(1, chan):
        partner(p).wait()
    everything = jnp.sum(square[...], axis=0)[:1]
    norm_ref[...] = jnp.sqrt(jnp.sum(everything, axis=1, keepdims=True))


def copy_kernel(*refs):
    count = (len(refs) - 2) // 3
    staged = refs[2 * count : 3 * count]
    inward = [
        pltpu.make_async_copy(refs[i], staged[i], refs[-2].at[i]) for i in range(count)
    ]
    outward = [
        pltpu.make_async_copy(staged[i], refs[count + i], refs[-1].at[i]) for i in range(count)
    ]
    for copy in inward:
        copy.start()
    for i in range(count):
        inward[i].wait()
        outward[i].start()
    for copy in outward:
        copy.wait()


def on_device(ctx, chan, query_in, key_in, value_in, grad_out, residue, decay_rate):
    rows, channels = query_in.shape
    modes = residue.shape[0]
    tiles = channels // LANES
    block = rows // SUBS
    chips = ctx // 2
    half = modes // 2
    f32 = jnp.float32
    vmem = pl.BlockSpec(memory_space=pltpu.VMEM)
    dma = pltpu.SemaphoreType.DMA

    def buffer(*shape):
        return pltpu.VMEM(shape, f32)

    shapes = (
        [jax.ShapeDtypeStruct((rows, channels), jnp.bfloat16)] * 3
        + [jax.ShapeDtypeStruct((modes, channels), f32)] * 2
        + [jax.ShapeDtypeStruct((1, 1), f32)]
    )
    found = pl.pallas_call(
        functools.partial(kernel, ctx, chan, rows * ctx),
        in_specs=[vmem] * 6,
        out_specs=[vmem] * 6,
        out_shape=shapes,
        scratch_shapes=[
            buffer(tiles, rows, LANES),
            buffer(tiles, rows, LANES),
            buffer(tiles, modes, LANES),
            buffer(tiles, modes, LANES),
            buffer(tiles, modes, LANES),
            buffer(tiles, block, SUBS, LANES),
            buffer(2, tiles, modes, LANES),
            buffer(modes, tiles, SUBS, LANES),
            buffer(modes, tiles, SUBS, LANES),
            buffer(tiles, block, SUBS, LANES),
            buffer(tiles, block, SUBS, LANES),
            buffer(modes, tiles, LANES),
            buffer(modes, 6 * tiles, LANES),
            buffer(modes, 6 * tiles, LANES),
            buffer(half, 6 * tiles, LANES),
            buffer(chips, 6 * tiles, LANES),
            buffer(chips, 2 * tiles, LANES),
            buffer(modes, 2 * tiles, LANES),
            buffer(modes, 2 * tiles, LANES),
            buffer(2 * tiles, LANES),
            buffer(modes, 2 * tiles, LANES),
            buffer(chan, SUBS, LANES),
            dma, dma, dma((half,)), dma((chips,)), dma((ctx,)), dma((modes,)),
            dma, dma, dma((ctx,)), dma((modes,)), dma((chan,)), dma((chan,)),
        ],
        compiler_params=pltpu.CompilerParams(collective_id=0, has_side_effects=True),
        name="hyena",
    )(query_in, key_in, value_in, grad_out, residue, decay_rate)
    anywhere = pl.BlockSpec(memory_space=pl.ANY)
    count = len(shapes) - 1
    placed = pl.pallas_call(
        copy_kernel,
        in_specs=[anywhere] * count,
        out_specs=[anywhere] * count,
        out_shape=shapes[:count],
        scratch_shapes=[pltpu.VMEM(leaf.shape, leaf.dtype) for leaf in shapes[:count]]
        + [dma((count,)), dma((count,))],
        name="place",
    )(*found[:count])
    return (*placed, found[count].reshape(()))


def solution(mesh):
    return jax.shard_map(
        functools.partial(on_device, mesh.shape["ctx"], mesh.shape["chan"]),
        mesh=mesh,
        in_specs=(P("ctx", "chan"),) * 4 + (P(None, "chan"),) * 2,
        out_specs=(P("ctx", "chan"),) * 3 + (P(None, "chan"),) * 2 + (P(),),
        check_vma=False,
    )
```

```python
import functools

import jax
import jax.numpy as jnp
from jax import lax
from jax.experimental import pallas as pl
from jax.experimental.pallas import tpu as pltpu
from jax.sharding import PartitionSpec as P

MESH = pl.DeviceIdType.MESH
LANES = 128
SUBS = 8
GROUP = 4
UNROLL = 16


def kernel(
    ctx, chan, positions,
    query_ref, key_ref, value_ref, grad_ref, res_ref, rate_ref,
    gq_ref, gk_ref, gv_ref, gres_ref, grate_ref, norm_ref,
    mixed, gmix, factors, rates, residues, lags, enters, leaves, convs, gconvs, spans,
    sums, twin, chipsum, inbox, outbox, heard, edges, total, answer, square,
    send0, recv0, send1, recv1, send2, recv2, send3, recv3, send4, recv4, send5, recv5,
):
    modes, channels = res_ref.shape
    tiles = channels // LANES
    rows = query_ref.shape[0]
    block = rows // SUBS
    chips = ctx // 2
    half = modes // 2
    stride = chips // half
    me = lax.axis_index("ctx")
    mine = lax.axis_index("chan")
    chip = me // 2
    core = lax.rem(me, 2)
    sibling = 2 * chip + 1 - core
    owned = chip // stride
    mode = core * half + owned
    own_half = pl.ds(core * half, half)
    other_half = pl.ds((1 - core) * half, half)
    f32 = jnp.float32

    barrier = pltpu.get_barrier_semaphore()

    @pl.loop(1, ctx, unroll=ctx <= UNROLL)
    def _(p):
        pl.semaphore_signal(
            barrier, inc=1, device_id=(lax.rem(me + p, ctx), mine), device_id_type=MESH
        )

    for p in range(1, chan):
        pl.semaphore_signal(
            barrier, inc=1, device_id=(me, lax.rem(mine + p, chan)), device_id_type=MESH
        )

    sub = lax.broadcasted_iota(jnp.int32, (SUBS, LANES), 0)
    before = sub.astype(f32) * float(block)
    after = (SUBS - 1 - sub).astype(f32) * float(block)

    def lanes_of(t):
        return pl.ds(pl.multiple_of(t * LANES, LANES), LANES)

    def blocks_of(ref, t):
        return [ref[t, pl.ds(i, SUBS, stride=block), :] for i in range(block)]

    def row_of(ref, m, t):
        return jnp.broadcast_to(ref[t, pl.ds(m, 1), :], (SUBS, LANES))

    @pl.loop(0, tiles)
    def _(t):
        lanes = lanes_of(t)
        mixed[t] = key_ref[:, lanes].astype(f32) * value_ref[:, lanes].astype(f32)
        gmix[t] = grad_ref[:, lanes].astype(f32) * query_ref[:, lanes].astype(f32)
        rates[t] = rate_ref[:, lanes]
        residues[t] = res_ref[:, lanes]
        factors[t] = jnp.exp(-rates[t])
        x = blocks_of(mixed, t)
        g = blocks_of(gmix, t)
        factor = factors[t]
        power = jnp.ones_like(factor)
        lag_res = jnp.zeros_like(factor)
        lag_rate = jnp.zeros_like(factor)
        for j in range(block):
            products = x[0] * g[j]
            for i in range(1, block - j):
                products = products + x[i] * g[i + j]
            term = power * jnp.sum(products, axis=0, keepdims=True)
            lag_res = lag_res + term
            lag_rate = lag_rate + float(j) * term
            power = power * factor
        lags[0, t] = lag_res
        lags[1, t] = lag_rate

        @pl.loop(0, modes // GROUP)
        def _(at):
            for lane in range(GROUP):
                m = at * GROUP + lane
                f = row_of(factors, m, t)
                head = x[0] * f
                head1 = head
                tail = g[block - 1]
                tail1 = jnp.zeros_like(tail)
                for i in range(1, block):
                    head = (head + x[i]) * f
                    head1 = head1 * f + head
                    tail1 = (tail1 + tail) * f
                    tail = tail * f + g[block - 1 - i]
                rate = rates[t, pl.ds(m, 1), :]
                step = jnp.exp(rate * -float(block))
                up, down, weight = head, tail, jnp.broadcast_to(step, (SUBS, LANES))
                for shift in (1, 2, 4):
                    up = up + jnp.where(sub >= shift, weight * pltpu.roll(up, shift, 0), 0.0)
                    down = down + jnp.where(
                        sub < SUBS - shift, weight * pltpu.roll(down, SUBS - shift, 0), 0.0
                    )
                    weight = weight * weight
                enter = jnp.where(sub >= 1, pltpu.roll(up, 1, 0), 0.0)
                leave = jnp.where(sub < SUBS - 1, pltpu.roll(down, SUBS - 1, 0), 0.0)
                enters[m, t] = enter
                leaves[m, t] = leave
                moment = jnp.exp(-rate * after) * (head1 + after * head)
                gmoment = jnp.exp(-rate * before) * (tail1 + before * tail)
                cross = head * leave
                cross1 = head1 * leave + enter * (tail1 + float(block) * step * leave)
                found = (
                    up[SUBS - 1 :],
                    down[:1],
                    jnp.sum(moment, axis=0, keepdims=True),
                    jnp.sum(gmoment, axis=0, keepdims=True),
                    jnp.sum(cross, axis=0, keepdims=True) + lags[0, t, pl.ds(m, 1), :],
                    jnp.sum(cross1, axis=0, keepdims=True) + lags[1, t, pl.ds(m, 1), :],
                )
                for at_row, row in enumerate(found):
                    sums[m, pl.ds(at_row * tiles + t, 1), :] = row
                spans[m, pl.ds(t, 1), :] = weight[:1]

    pl.semaphore_wait(barrier, ctx - 1 + chan - 1)

    def remote(src, dst, send, recv, target):
        return pltpu.make_async_remote_copy(
            src_ref=src, dst_ref=dst, send_sem=send, recv_sem=recv,
            device_id=(target, mine), device_id_type=MESH,
        )

    def pair_up():
        return remote(sums.at[other_half], twin.at[other_half], send0, recv0, sibling)

    def pair_rest():
        return remote(sums.at[own_half], twin.at[own_half], send3, recv3, sibling)

    def ask(j, slot, at):
        return remote(
            chipsum.at[j], inbox.at[slot], send1.at[j], recv1.at[slot], 2 * at + core
        )

    def reply(d, slot):
        return remote(outbox.at[d // 2], heard.at[slot], send2.at[d], recv2.at[slot], d)

    def spread(d, slot):
        return remote(total, answer.at[slot], send4.at[d], recv4.at[slot], d)

    def if_owner(then, otherwise=None):
        if stride == 1:
            then()
            return
        owner = lax.rem(chip, stride) == 0
        pl.when(owner)(then)
        if otherwise is not None:
            pl.when(jnp.logical_not(owner))(otherwise)

    def each(count, start, act):
        @pl.loop(1, count, unroll=count <= UNROLL)
        def _(p):
            act(lax.rem(start + p, count))

    def part(ref, k):
        return ref[:, k * tiles : (k + 1) * tiles, :]

    pair_up().start()
    pair_rest().start()
    first = core == 0
    span = spans[own_half]

    def ordered(k):
        here = sums[own_half, k * tiles : (k + 1) * tiles, :]
        there = twin[own_half, k * tiles : (k + 1) * tiles, :]
        return jnp.where(first, here, there), jnp.where(first, there, here)

    pair_up().wait_recv()
    (xa, xb), (ga, gb), (ma, mb), (na, nb), (ra, rb), (qa, qb) = [ordered(k) for k in range(6)]
    joined = (
        span * xa + xb,
        ga + span * gb,
        span * (ma + float(rows) * xa) + mb,
        na + span * (nb + float(rows) * gb),
        ra + rb + xa * gb,
        qa + qb + ma * gb + xa * nb,
    )
    for k, found in enumerate(joined):
        chipsum[:, k * tiles : (k + 1) * tiles, :] = found
    each(half, owned, lambda j: ask(j, chip, j * stride).start())
    if_owner(lambda: None, lambda: ask(owned, chip, owned * stride).start())

    @pl.loop(0, tiles)
    def _(t):
        x = blocks_of(mixed, t)
        g = blocks_of(gmix, t)
        factor = factors[t]
        power = residues[t]
        h = []
        for j in range(block):
            tap = jnp.sum(power, axis=0, keepdims=True)
            h.append(jnp.broadcast_to(tap, (SUBS, LANES)))
            power = power * factor
        for i in range(block):
            acc = h[0] * x[i]
            for j in range(1, i + 1):
                acc = acc + h[j] * x[i - j]
            convs[t, i] = acc
            acc = h[0] * g[i]
            for j in range(1, block - i):
                acc = acc + h[j] * g[i + j]
            gconvs[t, i] = acc

    def owner_work():
        inbox[chip] = chipsum[owned]
        each(chips, chip, lambda h: ask(owned, h, h).wait_recv())
        span2 = spans[mode] * spans[mode]
        enter = jnp.zeros_like(span2)
        leave = jnp.zeros_like(span2)
        for h in range(chips):
            outbox[h, 0:tiles, :] = enter
            enter = span2 * enter + inbox[h, 0:tiles, :]
            back = chips - 1 - h
            outbox[back, tiles : 2 * tiles, :] = leave
            leave = span2 * leave + inbox[back, tiles : 2 * tiles, :]
        each(ctx, me, lambda d: reply(d, mode).start())
        heard[mode] = outbox[chip]
        enter = part(outbox, 0)
        leave = part(outbox, 1)
        res_total = part(inbox, 4) + part(inbox, 0) * leave
        rate_total = (
            part(inbox, 5)
            + part(inbox, 2) * leave
            + enter * (part(inbox, 3) + float(2 * rows) * span2 * leave)
        )
        total[0:tiles, :] = jnp.sum(res_total, axis=0)
        total[tiles : 2 * tiles, :] = jnp.sum(rate_total, axis=0)
        each(ctx, me, lambda d: spread(d, mode).start())
        answer[mode] = total[...]

    if_owner(owner_work, lambda: reply(me, mode).wait_recv())
    pair_rest().wait_recv()
    each(modes, mode, lambda m: reply(me, m).wait_recv())

    enter = part(heard, 0)
    leave = part(heard, 1)
    edges[:, 0:tiles, :] = jnp.where(first, enter, spans[...] * enter + part(twin, 0))
    edges[:, tiles : 2 * tiles, :] = jnp.where(first, spans[...] * leave + part(twin, 1), leave)

    def finish(t):
        lanes = lanes_of(t)

        def forward(at, held):
            conv = list(held)
            for lane in range(GROUP):
                m = at * GROUP + lane
                f = row_of(factors, m, t)
                rate = rates[t, pl.ds(m, 1), :]
                res = residues[t, pl.ds(m, 1), :]
                into = edges[m, pl.ds(t, 1), :]
                z = res * (enters[m, t] + jnp.exp(-rate * before) * into)
                for i in range(block):
                    conv[i] = conv[i] + z
                    if i < block - 1:
                        z = z * f
            return tuple(conv)

        def backward(at, held):
            gconv = list(held)
            for lane in range(GROUP):
                m = at * GROUP + lane
                f = row_of(factors, m, t)
                rate = rates[t, pl.ds(m, 1), :]
                res = residues[t, pl.ds(m, 1), :]
                out = edges[m, pl.ds(tiles + t, 1), :]
                y = (res * f) * (leaves[m, t] + jnp.exp(-rate * after) * out)
                for i in range(block - 1, -1, -1):
                    gconv[i] = gconv[i] + y
                    if i > 0:
                        y = y * f
            return tuple(gconv)

        steps = modes // GROUP
        conv = lax.fori_loop(0, steps, forward, tuple(convs[t, i] for i in range(block)))
        gconv = lax.fori_loop(0, steps, backward, tuple(gconvs[t, i] for i in range(block)))
        for i in range(block):
            mixed[t, pl.ds(i, SUBS, stride=block), :] = conv[i]
            gmix[t, pl.ds(i, SUBS, stride=block), :] = gconv[i]
        whole = mixed[t]
        gwhole = gmix[t]
        gq_ref[:, lanes] = (grad_ref[:, lanes].astype(f32) * whole).astype(jnp.bfloat16)
        gk_ref[:, lanes] = (gwhole * value_ref[:, lanes].astype(f32)).astype(jnp.bfloat16)
        gv_ref[:, lanes] = (gwhole * key_ref[:, lanes].astype(f32)).astype(jnp.bfloat16)

    pl.loop(0, tiles // 4)(finish)

    if_owner(lambda: None, lambda: spread(me, mode).wait_recv())
    each(modes, mode, lambda m: spread(me, m).wait_recv())

    squares = jnp.zeros((1, LANES), f32)
    for t in range(tiles):
        lanes = slice(t * LANES, (t + 1) * LANES)
        grad_res = answer[:, t, :] / positions
        grad_rate = (
            -rate_ref[:, lanes] * res_ref[:, lanes] * answer[:, tiles + t, :] / positions
        )
        gres_ref[:, lanes] = grad_res
        grate_ref[:, lanes] = grad_rate
        squares = squares + jnp.sum(
            grad_res * grad_res + grad_rate * grad_rate, axis=0, keepdims=True
        )
    square[0] = jnp.broadcast_to(squares, (SUBS, LANES))

    def partner(p):
        return pltpu.make_async_remote_copy(
            src_ref=square.at[0],
            dst_ref=square.at[p],
            send_sem=send5.at[p],
            recv_sem=recv5.at[p],
            device_id=(me, lax.rem(mine + p, chan)),
            device_id_type=MESH,
        )

    for p in range(1, chan):
        partner(p).start()

    pl.loop(tiles // 4, tiles)(finish)

    pair_up().wait_send()
    pair_rest().wait_send()
    each(half, owned, lambda j: ask(j, chip, j * stride).wait_send())

    def owner_drain():
        each(ctx, me, lambda d: reply(d, mode).wait_send())
        each(ctx, me, lambda d: spread(d, mode).wait_send())

    def other_drain():
        ask(owned, chip, owned * stride).wait_send()

    if_owner(owner_drain, other_drain)

    for p in range(1, chan):
        partner(p).wait()
    everything = jnp.sum(square[...], axis=0)[:1]
    norm_ref[...] = jnp.sqrt(jnp.sum(everything, axis=1, keepdims=True))


def copy_kernel(*refs):
    count = (len(refs) - 2) // 3
    staged = refs[2 * count : 3 * count]
    inward = [
        pltpu.make_async_copy(refs[i], staged[i], refs[-2].at[i]) for i in range(count)
    ]
    outward = [
        pltpu.make_async_copy(staged[i], refs[count + i], refs[-1].at[i]) for i in range(count)
    ]
    for copy in inward:
        copy.start()
    for i in range(count):
        inward[i].wait()
        outward[i].start()
    for copy in outward:
        copy.wait()


def on_device(ctx, chan, query_in, key_in, value_in, grad_out, residue, decay_rate):
    rows, channels = query_in.shape
    modes = residue.shape[0]
    tiles = channels // LANES
    block = rows // SUBS
    chips = ctx // 2
    half = modes // 2
    f32 = jnp.float32
    vmem = pl.BlockSpec(memory_space=pltpu.VMEM)
    dma = pltpu.SemaphoreType.DMA

    def buffer(*shape):
        return pltpu.VMEM(shape, f32)

    shapes = (
        [jax.ShapeDtypeStruct((rows, channels), jnp.bfloat16)] * 3
        + [jax.ShapeDtypeStruct((modes, channels), f32)] * 2
        + [jax.ShapeDtypeStruct((1, 1), f32)]
    )
    found = pl.pallas_call(
        functools.partial(kernel, ctx, chan, rows * ctx),
        in_specs=[vmem] * 6,
        out_specs=[vmem] * 6,
        out_shape=shapes,
        scratch_shapes=[
            buffer(tiles, rows, LANES),
            buffer(tiles, rows, LANES),
            buffer(tiles, modes, LANES),
            buffer(tiles, modes, LANES),
            buffer(tiles, modes, LANES),
            buffer(2, tiles, modes, LANES),
            buffer(modes, tiles, SUBS, LANES),
            buffer(modes, tiles, SUBS, LANES),
            buffer(tiles, block, SUBS, LANES),
            buffer(tiles, block, SUBS, LANES),
            buffer(modes, tiles, LANES),
            buffer(modes, 6 * tiles, LANES),
            buffer(modes, 6 * tiles, LANES),
            buffer(half, 6 * tiles, LANES),
            buffer(chips, 6 * tiles, LANES),
            buffer(chips, 2 * tiles, LANES),
            buffer(modes, 2 * tiles, LANES),
            buffer(modes, 2 * tiles, LANES),
            buffer(2 * tiles, LANES),
            buffer(modes, 2 * tiles, LANES),
            buffer(chan, SUBS, LANES),
            dma, dma, dma((half,)), dma((chips,)), dma((ctx,)), dma((modes,)),
            dma, dma, dma((ctx,)), dma((modes,)), dma((chan,)), dma((chan,)),
        ],
        compiler_params=pltpu.CompilerParams(collective_id=0, has_side_effects=True),
        name="hyena",
    )(query_in, key_in, value_in, grad_out, residue, decay_rate)
    anywhere = pl.BlockSpec(memory_space=pl.ANY)
    count = len(shapes) - 1
    placed = pl.pallas_call(
        copy_kernel,
        in_specs=[anywhere] * count,
        out_specs=[anywhere] * count,
        out_shape=shapes[:count],
        scratch_shapes=[pltpu.VMEM(leaf.shape, leaf.dtype) for leaf in shapes[:count]]
        + [dma((count,)), dma((count,))],
        name="place",
    )(*found[:count])
    return (*placed, found[count].reshape(()))


def solution(mesh):
    return jax.shard_map(
        functools.partial(on_device, mesh.shape["ctx"], mesh.shape["chan"]),
        mesh=mesh,
        in_specs=(P("ctx", "chan"),) * 4 + (P(None, "chan"),) * 2,
        out_specs=(P("ctx", "chan"),) * 3 + (P(None, "chan"),) * 2 + (P(),),
        check_vma=False,
    )
```

```python
import functools

import jax
import jax.numpy as jnp
from jax import lax
from jax.experimental import pallas as pl
from jax.experimental.pallas import tpu as pltpu
from jax.sharding import PartitionSpec as P

MESH = pl.DeviceIdType.MESH
LANES = 128
SUBS = 8
GROUP = 4
UNROLL = 16


def kernel(
    ctx, chan, positions,
    query_ref, key_ref, value_ref, grad_ref, res_ref, rate_ref,
    gq_ref, gk_ref, gv_ref, gres_ref, grate_ref, norm_ref,
    mixed, gmix, factors, rates, residues, lags, enters, leaves, convs, gconvs, spans,
    sums, twin, chipsum, inbox, outbox, heard, edges, total, answer, square,
    send0, recv0, send1, recv1, send2, recv2, send3, recv3, send4, recv4, send5, recv5,
):
    modes, channels = res_ref.shape
    tiles = channels // LANES
    rows = query_ref.shape[0]
    block = rows // SUBS
    chips = ctx // 2
    half = modes // 2
    stride = chips // half
    me = lax.axis_index("ctx")
    mine = lax.axis_index("chan")
    chip = me // 2
    core = lax.rem(me, 2)
    sibling = 2 * chip + 1 - core
    owned = chip // stride
    mode = core * half + owned
    own_half = pl.ds(core * half, half)
    other_half = pl.ds((1 - core) * half, half)
    f32 = jnp.float32

    barrier = pltpu.get_barrier_semaphore()

    @pl.loop(1, ctx, unroll=ctx <= UNROLL)
    def _(p):
        pl.semaphore_signal(
            barrier, inc=1, device_id=(lax.rem(me + p, ctx), mine), device_id_type=MESH
        )

    for p in range(1, chan):
        pl.semaphore_signal(
            barrier, inc=1, device_id=(me, lax.rem(mine + p, chan)), device_id_type=MESH
        )

    sub = lax.broadcasted_iota(jnp.int32, (SUBS, LANES), 0)
    before = sub.astype(f32) * float(block)
    after = (SUBS - 1 - sub).astype(f32) * float(block)

    def lanes_of(t):
        return pl.ds(pl.multiple_of(t * LANES, LANES), LANES)

    def blocks_of(ref, t):
        return [ref[t, pl.ds(i, SUBS, stride=block), :] for i in range(block)]

    def row_of(ref, m, t):
        return jnp.broadcast_to(ref[t, pl.ds(m, 1), :], (SUBS, LANES))

    @pl.loop(0, tiles)
    def _(t):
        lanes = lanes_of(t)
        mixed[t] = key_ref[:, lanes].astype(f32) * value_ref[:, lanes].astype(f32)
        gmix[t] = grad_ref[:, lanes].astype(f32) * query_ref[:, lanes].astype(f32)
        rates[t] = rate_ref[:, lanes]
        residues[t] = res_ref[:, lanes]
        factors[t] = jnp.exp(-rates[t])
        x = blocks_of(mixed, t)
        g = blocks_of(gmix, t)
        factor = factors[t]
        power = jnp.ones_like(factor)
        lag_res = jnp.zeros_like(factor)
        lag_rate = jnp.zeros_like(factor)
        for j in range(block):
            products = x[0] * g[j]
            for i in range(1, block - j):
                products = products + x[i] * g[i + j]
            term = power * jnp.sum(products, axis=0, keepdims=True)
            lag_res = lag_res + term
            lag_rate = lag_rate + float(j) * term
            power = power * factor
        lags[0, t] = lag_res
        lags[1, t] = lag_rate

        @pl.loop(0, modes // GROUP)
        def _(at):
            for lane in range(GROUP):
                m = at * GROUP + lane
                f = row_of(factors, m, t)
                head = x[0] * f
                head1 = head
                tail = g[block - 1]
                tail1 = jnp.zeros_like(tail)
                for i in range(1, block):
                    head = (head + x[i]) * f
                    head1 = head1 * f + head
                    tail1 = (tail1 + tail) * f
                    tail = tail * f + g[block - 1 - i]
                rate = rates[t, pl.ds(m, 1), :]
                step = jnp.exp(rate * -float(block))
                up, down, weight = head, tail, jnp.broadcast_to(step, (SUBS, LANES))
                for shift in (1, 2, 4):
                    up = up + jnp.where(sub >= shift, weight * pltpu.roll(up, shift, 0), 0.0)
                    down = down + jnp.where(
                        sub < SUBS - shift, weight * pltpu.roll(down, SUBS - shift, 0), 0.0
                    )
                    weight = weight * weight
                enter = jnp.where(sub >= 1, pltpu.roll(up, 1, 0), 0.0)
                leave = jnp.where(sub < SUBS - 1, pltpu.roll(down, SUBS - 1, 0), 0.0)
                enters[m, t] = enter
                leaves[m, t] = leave
                moment = jnp.exp(-rate * after) * (head1 + after * head)
                gmoment = jnp.exp(-rate * before) * (tail1 + before * tail)
                cross = head * leave
                cross1 = head1 * leave + enter * (tail1 + float(block) * step * leave)
                found = (
                    up[SUBS - 1 :],
                    down[:1],
                    jnp.sum(moment, axis=0, keepdims=True),
                    jnp.sum(gmoment, axis=0, keepdims=True),
                    jnp.sum(cross, axis=0, keepdims=True) + lags[0, t, pl.ds(m, 1), :],
                    jnp.sum(cross1, axis=0, keepdims=True) + lags[1, t, pl.ds(m, 1), :],
                )
                for at_row, row in enumerate(found):
                    sums[m, pl.ds(at_row * tiles + t, 1), :] = row
                spans[m, pl.ds(t, 1), :] = weight[:1]

    pl.semaphore_wait(barrier, ctx - 1 + chan - 1)

    def remote(src, dst, send, recv, target):
        return pltpu.make_async_remote_copy(
            src_ref=src, dst_ref=dst, send_sem=send, recv_sem=recv,
            device_id=(target, mine), device_id_type=MESH,
        )

    def pair_up():
        return remote(sums.at[other_half], twin.at[other_half], send0, recv0, sibling)

    def pair_rest():
        return remote(sums.at[own_half], twin.at[own_half], send3, recv3, sibling)

    def ask(j, slot, at):
        return remote(
            chipsum.at[j], inbox.at[slot], send1.at[j], recv1.at[slot], 2 * at + core
        )

    def reply(d, slot):
        return remote(outbox.at[d // 2], heard.at[slot], send2.at[d], recv2.at[slot], d)

    def spread(d, slot):
        return remote(total, answer.at[slot], send4.at[d], recv4.at[slot], d)

    def if_owner(then, otherwise=None):
        if stride == 1:
            then()
            return
        owner = lax.rem(chip, stride) == 0
        pl.when(owner)(then)
        if otherwise is not None:
            pl.when(jnp.logical_not(owner))(otherwise)

    def each(count, start, act):
        @pl.loop(1, count, unroll=count <= UNROLL)
        def _(p):
            act(lax.rem(start + p, count))

    def part(ref, k):
        return ref[:, k * tiles : (k + 1) * tiles, :]

    pair_up().start()
    pair_rest().start()
    first = core == 0
    span = spans[own_half]

    def ordered(k):
        here = sums[own_half, k * tiles : (k + 1) * tiles, :]
        there = twin[own_half, k * tiles : (k + 1) * tiles, :]
        return jnp.where(first, here, there), jnp.where(first, there, here)

    pair_up().wait_recv()
    (xa, xb), (ga, gb), (ma, mb), (na, nb), (ra, rb), (qa, qb) = [ordered(k) for k in range(6)]
    joined = (
        span * xa + xb,
        ga + span * gb,
        span * (ma + float(rows) * xa) + mb,
        na + span * (nb + float(rows) * gb),
        ra + rb + xa * gb,
        qa + qb + ma * gb + xa * nb,
    )
    for k, found in enumerate(joined):
        chipsum[:, k * tiles : (k + 1) * tiles, :] = found
    each(half, owned, lambda j: ask(j, chip, j * stride).start())
    if_owner(lambda: None, lambda: ask(owned, chip, owned * stride).start())

    @pl.loop(0, tiles)
    def _(t):
        x = blocks_of(mixed, t)
        g = blocks_of(gmix, t)
        factor = factors[t]
        power = residues[t]
        h = []
        for j in range(block):
            tap = jnp.sum(power, axis=0, keepdims=True)
            h.append(jnp.broadcast_to(tap, (SUBS, LANES)))
            power = power * factor
        for i in range(block):
            acc = h[0] * x[i]
            for j in range(1, i + 1):
                acc = acc + h[j] * x[i - j]
            convs[t, i] = acc
            acc = h[0] * g[i]
            for j in range(1, block - i):
                acc = acc + h[j] * g[i + j]
            gconvs[t, i] = acc

    def owner_work():
        inbox[chip] = chipsum[owned]
        each(chips, chip, lambda h: ask(owned, h, h).wait_recv())
        span2 = spans[mode] * spans[mode]
        enter = jnp.zeros_like(span2)
        leave = jnp.zeros_like(span2)
        for h in range(chips):
            outbox[h, 0:tiles, :] = enter
            enter = span2 * enter + inbox[h, 0:tiles, :]
            back = chips - 1 - h
            outbox[back, tiles : 2 * tiles, :] = leave
            leave = span2 * leave + inbox[back, tiles : 2 * tiles, :]
        each(ctx, me, lambda d: reply(d, mode).start())
        heard[mode] = outbox[chip]
        enter = part(outbox, 0)
        leave = part(outbox, 1)
        res_total = part(inbox, 4) + part(inbox, 0) * leave
        rate_total = (
            part(inbox, 5)
            + part(inbox, 2) * leave
            + enter * (part(inbox, 3) + float(2 * rows) * span2 * leave)
        )
        total[0:tiles, :] = jnp.sum(res_total, axis=0)
        total[tiles : 2 * tiles, :] = jnp.sum(rate_total, axis=0)
        each(ctx, me, lambda d: spread(d, mode).start())
        answer[mode] = total[...]

    if_owner(owner_work, lambda: reply(me, mode).wait_recv())
    pair_rest().wait_recv()
    each(modes, mode, lambda m: reply(me, m).wait_recv())

    enter = part(heard, 0)
    leave = part(heard, 1)
    edges[:, 0:tiles, :] = jnp.where(first, enter, spans[...] * enter + part(twin, 0))
    edges[:, tiles : 2 * tiles, :] = jnp.where(first, spans[...] * leave + part(twin, 1), leave)

    def finish(t):
        lanes = lanes_of(t)

        def forward(at, held):
            conv = list(held)
            for lane in range(GROUP):
                m = at * GROUP + lane
                f = row_of(factors, m, t)
                rate = rates[t, pl.ds(m, 1), :]
                res = residues[t, pl.ds(m, 1), :]
                into = edges[m, pl.ds(t, 1), :]
                z = res * (enters[m, t] + jnp.exp(-rate * before) * into)
                for i in range(block):
                    conv[i] = conv[i] + z
                    if i < block - 1:
                        z = z * f
            return tuple(conv)

        def backward(at, held):
            gconv = list(held)
            for lane in range(GROUP):
                m = at * GROUP + lane
                f = row_of(factors, m, t)
                rate = rates[t, pl.ds(m, 1), :]
                res = residues[t, pl.ds(m, 1), :]
                out = edges[m, pl.ds(tiles + t, 1), :]
                y = (res * f) * (leaves[m, t] + jnp.exp(-rate * after) * out)
                for i in range(block - 1, -1, -1):
                    gconv[i] = gconv[i] + y
                    if i > 0:
                        y = y * f
            return tuple(gconv)

        steps = modes // GROUP
        conv = lax.fori_loop(0, steps, forward, tuple(convs[t, i] for i in range(block)))
        gconv = lax.fori_loop(0, steps, backward, tuple(gconvs[t, i] for i in range(block)))
        for i in range(block):
            mixed[t, pl.ds(i, SUBS, stride=block), :] = conv[i]
            gmix[t, pl.ds(i, SUBS, stride=block), :] = gconv[i]
        whole = mixed[t]
        gwhole = gmix[t]
        gq_ref[:, lanes] = (grad_ref[:, lanes].astype(f32) * whole).astype(jnp.bfloat16)
        gk_ref[:, lanes] = (gwhole * value_ref[:, lanes].astype(f32)).astype(jnp.bfloat16)
        gv_ref[:, lanes] = (gwhole * key_ref[:, lanes].astype(f32)).astype(jnp.bfloat16)


    if_owner(lambda: None, lambda: spread(me, mode).wait_recv())
    each(modes, mode, lambda m: spread(me, m).wait_recv())

    squares = jnp.zeros((1, LANES), f32)
    for t in range(tiles):
        lanes = slice(t * LANES, (t + 1) * LANES)
        grad_res = answer[:, t, :] / positions
        grad_rate = (
            -rate_ref[:, lanes] * res_ref[:, lanes] * answer[:, tiles + t, :] / positions
        )
        gres_ref[:, lanes] = grad_res
        grate_ref[:, lanes] = grad_rate
        squares = squares + jnp.sum(
            grad_res * grad_res + grad_rate * grad_rate, axis=0, keepdims=True
        )
    square[0] = jnp.broadcast_to(squares, (SUBS, LANES))

    def partner(p):
        return pltpu.make_async_remote_copy(
            src_ref=square.at[0],
            dst_ref=square.at[p],
            send_sem=send5.at[p],
            recv_sem=recv5.at[p],
            device_id=(me, lax.rem(mine + p, chan)),
            device_id_type=MESH,
        )

    for p in range(1, chan):
        partner(p).start()

    pl.loop(0, tiles)(finish)

    pair_up().wait_send()
    pair_rest().wait_send()
    each(half, owned, lambda j: ask(j, chip, j * stride).wait_send())

    def owner_drain():
        each(ctx, me, lambda d: reply(d, mode).wait_send())
        each(ctx, me, lambda d: spread(d, mode).wait_send())

    def other_drain():
        ask(owned, chip, owned * stride).wait_send()

    if_owner(owner_drain, other_drain)

    for p in range(1, chan):
        partner(p).wait()
    everything = jnp.sum(square[...], axis=0)[:1]
    norm_ref[...] = jnp.sqrt(jnp.sum(everything, axis=1, keepdims=True))


def copy_kernel(*refs):
    count = (len(refs) - 2) // 3
    staged = refs[2 * count : 3 * count]
    inward = [
        pltpu.make_async_copy(refs[i], staged[i], refs[-2].at[i]) for i in range(count)
    ]
    outward = [
        pltpu.make_async_copy(staged[i], refs[count + i], refs[-1].at[i]) for i in range(count)
    ]
    for copy in inward:
        copy.start()
    for i in range(count):
        inward[i].wait()
        outward[i].start()
    for copy in outward:
        copy.wait()


def on_device(ctx, chan, query_in, key_in, value_in, grad_out, residue, decay_rate):
    rows, channels = query_in.shape
    modes = residue.shape[0]
    tiles = channels // LANES
    block = rows // SUBS
    chips = ctx // 2
    half = modes // 2
    f32 = jnp.float32
    vmem = pl.BlockSpec(memory_space=pltpu.VMEM)
    dma = pltpu.SemaphoreType.DMA

    def buffer(*shape):
        return pltpu.VMEM(shape, f32)

    shapes = (
        [jax.ShapeDtypeStruct((rows, channels), jnp.bfloat16)] * 3
        + [jax.ShapeDtypeStruct((modes, channels), f32)] * 2
        + [jax.ShapeDtypeStruct((1, 1), f32)]
    )
    found = pl.pallas_call(
        functools.partial(kernel, ctx, chan, rows * ctx),
        in_specs=[vmem] * 6,
        out_specs=[vmem] * 6,
        out_shape=shapes,
        scratch_shapes=[
            buffer(tiles, rows, LANES),
            buffer(tiles, rows, LANES),
            buffer(tiles, modes, LANES),
            buffer(tiles, modes, LANES),
            buffer(tiles, modes, LANES),
            buffer(2, tiles, modes, LANES),
            buffer(modes, tiles, SUBS, LANES),
            buffer(modes, tiles, SUBS, LANES),
            buffer(tiles, block, SUBS, LANES),
            buffer(tiles, block, SUBS, LANES),
            buffer(modes, tiles, LANES),
            buffer(modes, 6 * tiles, LANES),
            buffer(modes, 6 * tiles, LANES),
            buffer(half, 6 * tiles, LANES),
            buffer(chips, 6 * tiles, LANES),
            buffer(chips, 2 * tiles, LANES),
            buffer(modes, 2 * tiles, LANES),
            buffer(modes, 2 * tiles, LANES),
            buffer(2 * tiles, LANES),
            buffer(modes, 2 * tiles, LANES),
            buffer(chan, SUBS, LANES),
            dma, dma, dma((half,)), dma((chips,)), dma((ctx,)), dma((modes,)),
            dma, dma, dma((ctx,)), dma((modes,)), dma((chan,)), dma((chan,)),
        ],
        compiler_params=pltpu.CompilerParams(collective_id=0, has_side_effects=True),
        name="hyena",
    )(query_in, key_in, value_in, grad_out, residue, decay_rate)
    anywhere = pl.BlockSpec(memory_space=pl.ANY)
    count = len(shapes) - 1
    placed = pl.pallas_call(
        copy_kernel,
        in_specs=[anywhere] * count,
        out_specs=[anywhere] * count,
        out_shape=shapes[:count],
        scratch_shapes=[pltpu.VMEM(leaf.shape, leaf.dtype) for leaf in shapes[:count]]
        + [dma((count,)), dma((count,))],
        name="place",
    )(*found[:count])
    return (*placed, found[count].reshape(()))


def solution(mesh):
    return jax.shard_map(
        functools.partial(on_device, mesh.shape["ctx"], mesh.shape["chan"]),
        mesh=mesh,
        in_specs=(P("ctx", "chan"),) * 4 + (P(None, "chan"),) * 2,
        out_specs=(P("ctx", "chan"),) * 3 + (P(None, "chan"),) * 2 + (P(),),
        check_vma=False,
    )
```
